512 devices in a mesh: tok: 32 (over y, x), kv: 16 (over z, core).
Axes of the slice: x: 4, y: 8, z: 8, core: 2. Of those that a mesh axis runs over, the one named last changes fastest.
Arguments:
- hidden_in: bfloat16 [32768, 1024], P(('tok', 'kv')), may hold values from -12 to 12
- qkv_weight: bfloat16 [1024, 3, 1024], P(None, None, 'kv'), may hold values from -1 to 1
- stretch_len: int32 [48], replicated, may hold values from 1 to 1024, 32768 in all
- out_weight: bfloat16 [1024, 1024], P('kv'), may hold values from -0.1875 to 0.1875
- ln1_gain: float32 [1024], replicated, may hold values from 0.5 to 1.5
- ln1_bias: float32 [1024], replicated, may hold values from -3 to 3
- up_weight: bfloat16 [1024, 4096], P(None, 'kv'), may hold values from -0.1875 to 0.1875
- down_weight: bfloat16 [4096, 1024], P('kv'), may hold values from -0.09375 to 0.09375
- ln2_gain: float32 [1024], replicated, may hold values from 0.5 to 1.5
- ln2_bias: float32 [1024], replicated, may hold values from -3 to 3
- dec_query: bfloat16 [1024, 1024], P(('tok', 'kv')), may hold values from -12 to 12
- kv_cache: bfloat16 [2, 32, 96, 128, 1024], P(None, 'tok', 'kv'), may hold values from -12 to 12
- piece_req: int32 [32, 96], P('tok', 'kv'), may hold values from 0 to 31, as said below
- piece_used: int32 [32, 96], P('tok', 'kv'), may hold values from 0 to 128, as said below
Outputs:
- prefill_out: bfloat16 [32768, 1024], P(('tok', 'kv'))
- dec_out: bfloat16 [1024, 1024], P(('tok', 'kv'))
The draws below stay inside these ranges and needn't reach their ends.
Inputs may be any that keep to these rules, and one draw needn't show every extreme that they name: `piece_req`: every request of an index of tok owns at least one piece of that index with a nonzero count. `piece_used`: slots with a count of 0 hold no tokens.
All inputs are finite; a program needn't handle non-finite values.
Results may differ from the reference program's by a relative error of at most 0.017.
Values may be sent and summed in bfloat16 or wider, within the bound.
A program may use at most 64 MiB of HBM per device.

```python
import math
import jax
import jax.numpy as jnp
import numpy as np
from jax import lax

D = 1024
H = 16
HD = 64
FF = 4096
REACH = 256
BLK = 1024
PTOK = 32768
CLEN = 1024
NSEG = 48
PLEN = 128
PIECES_DEV = 6
RQ_DEV = 2
RQ_TOK = 32
REQ = 1024
SLOTS = 96
N_TOK = 32
N_KV = 16


def draw_hidden_in(key, part):
    normals = jax.random.normal(jax.random.fold_in(key, 11), (PTOK, D), jnp.float32)
    return jnp.clip(normals, -12.0, 12.0).astype(jnp.bfloat16)


def draw_qkv_weight(key, part):
    normals = jax.random.normal(jax.random.fold_in(key, 51), (D, 3, D), jnp.float32)
    scales = jnp.array([1.5, 1.0, 3.0], jnp.float32).reshape(1, 3, 1) / math.sqrt(D)
    return jnp.clip(normals * scales, -1.0, 1.0).astype(jnp.bfloat16)


def draw_dec_query(key, part):
    normals = 5.0 * jax.random.normal(jax.random.fold_in(key, 21), (REQ, D), jnp.float32)
    return jnp.clip(normals, -12.0, 12.0).astype(jnp.bfloat16)


def draw_kv_cache(key, part):
    normals = jax.random.normal(jax.random.fold_in(key, 31), (2, N_TOK, SLOTS, PLEN, D), jnp.float32)
    normals = normals * jnp.array([1.0, 3.0], jnp.float32).reshape(2, 1, 1, 1, 1)
    return jnp.clip(normals, -12.0, 12.0).astype(jnp.bfloat16)


def piece_table(key):
    table_key = jax.random.fold_in(key, 41)
    requests = RQ_DEV * N_KV
    slot_count = PIECES_DEV * N_KV
    slot_ids = jnp.arange(slot_count, dtype=jnp.int32)[None, :]
    candidates = jax.random.randint(jax.random.fold_in(table_key, 1), (N_TOK, slot_count, 3), 0, requests)
    skewed = jnp.min(candidates, axis=2)
    owners = jnp.where(slot_ids < requests, slot_ids, skewed)
    slot_kind = jax.random.randint(jax.random.fold_in(table_key, 2), (N_TOK, slot_count), 0, 3)
    partial_value = jax.random.randint(jax.random.fold_in(table_key, 3), (N_TOK, slot_count), 1, PLEN + 1)
    filled = jnp.where(slot_kind == 0, 0, jnp.where(slot_kind == 1, PLEN, partial_value))
    filled = jnp.where((slot_ids < requests) & (filled == 0), partial_value, filled)
    filled = jnp.where(slot_ids == 0, PLEN, filled)
    filled = jnp.where(slot_ids == slot_count - 1, 0, filled)
    ranks = jax.random.randint(jax.random.fold_in(table_key, 4), (N_TOK, slot_count), 0, 1 << 20) * slot_count + slot_ids
    shuffle = jnp.argsort(ranks, axis=1)
    owners = jnp.take_along_axis(owners, shuffle, axis=1)
    filled = jnp.take_along_axis(filled, shuffle, axis=1)
    return (owners.astype(jnp.int32), filled.astype(jnp.int32))


def draw_piece_req(key, part):
    return piece_table(key)[0]


def draw_piece_used(key, part):
    return piece_table(key)[1]


def block_levels(own_key, dims, shards, low, largest):
    def one(axis_at, shards_of):
        steps = jax.random.uniform(jax.random.fold_in(jax.random.fold_in(own_key, 6), axis_at), (shards_of,), jnp.float32, low / len(shards), largest / len(shards))
        return jnp.repeat(jnp.exp(steps), dims[axis_at] // shards_of).reshape((-1,) + (1,) * (len(dims) - axis_at - 1))

    loudness = one(*shards[0])
    for cut in shards[1:]:
        loudness = loudness * one(*cut)
    return loudness


def profile(number_of, total, most, slope):
    loads = [(1 << 20) // math.isqrt(rank ** slope) + 1 for rank in range(2, number_of + 1)]
    spare, holding = total - most - (number_of - 1), [1] * (number_of - 1)
    while spare > 0:
        movable = [i for i in range(number_of - 1) if holding[i] < most]
        mass, remaining = sum([loads[i] for i in movable]), spare
        for i in movable:
            extra = min(most - holding[i], max(1, remaining * loads[i] // mass), spare)
            holding[i] = holding[i] + extra
            spare = spare - extra
    return np.array([most] + holding)


def uneven(own_key, number_of, total, limit, lean):
    if number_of == 2:
        one = jax.random.randint(own_key, (), max(1, total - limit), min(limit, total - 1) + 1)
        return jnp.stack([one, total - one])
    tallies = jnp.asarray(profile(number_of, total, limit, lean), jnp.int32)
    couples = (number_of - 1) // 2
    donor, receiver = tallies[1:1 + 2 * couples:2], tallies[2:2 + 2 * couples:2]
    margin = jnp.minimum(donor - 1, limit - receiver)
    moved = jax.random.randint(jax.random.fold_in(own_key, 1), (couples,), 0, 1 << 20) % (margin + 1)
    tallies = tallies.at[1:1 + 2 * couples:2].set(donor - moved).at[2:2 + 2 * couples:2].set(receiver + moved)
    return tallies[jax.random.permutation(jax.random.fold_in(own_key, 2), number_of)]


def centred(key, extent, width, limit, shards=(), kind=jnp.bfloat16):
    values = width * jax.random.normal(key, extent, jnp.float32)
    if shards:
        values = values * block_levels(key, extent, shards, -0.22, 0.18)
    return jnp.clip(values, -limit, limit).astype(kind)


def setup_inputs(seed: int = 0) -> dict:
    seeds = jax.random.split(jax.random.key(seed), 15)
    hidden_in = draw_hidden_in(jax.random.fold_in(seeds[14], 71), 0)
    qkv_weight = draw_qkv_weight(jax.random.fold_in(seeds[14], 71), 0)
    stretch_len = uneven(seeds[2], NSEG, PTOK, CLEN, 2).astype(jnp.int32)
    out_weight = centred(seeds[3], (D, D), D ** -0.5, 0.1875, ((0, 16),))
    ln1_gain = jnp.clip(1.0 + 0.1 * jax.random.normal(seeds[4], (D,), jnp.float32), 0.5, 1.5)
    ln1_bias = centred(seeds[5], (D,), 0.5, 3.0, (), jnp.float32)
    up_weight = centred(seeds[6], (D, FF), D ** -0.5, 0.1875, ((1, 16),))
    down_weight = centred(seeds[7], (FF, D), FF ** -0.5, 0.09375, ((0, 16),))
    ln2_gain = jnp.clip(1.0 + 0.1 * jax.random.normal(seeds[8], (D,), jnp.float32), 0.5, 1.5)
    ln2_bias = centred(seeds[9], (D,), 0.5, 3.0, (), jnp.float32)
    dec_query = draw_dec_query(jax.random.fold_in(seeds[14], 71), 0)
    kv_cache = draw_kv_cache(jax.random.fold_in(seeds[14], 71), 0)
    piece_req = draw_piece_req(jax.random.fold_in(seeds[14], 71), 0)
    piece_used = draw_piece_used(jax.random.fold_in(seeds[14], 71), 0)
    return {"hidden_in": hidden_in, "qkv_weight": qkv_weight, "stretch_len": stretch_len, "out_weight": out_weight, "ln1_gain": ln1_gain, "ln1_bias": ln1_bias, "up_weight": up_weight, "down_weight": down_weight, "ln2_gain": ln2_gain, "ln2_bias": ln2_bias, "dec_query": dec_query, "kv_cache": kv_cache, "piece_req": piece_req, "piece_used": piece_used}


NEG_FILL = -1e+30
LN_EPS = 1e-05

def segment_ids(row_ids, stretch_len):
    stretch_ends = jnp.cumsum(stretch_len).astype(jnp.int32)
    return lax.optimization_barrier(jnp.sum((row_ids[:, None] >= stretch_ends[None, :]).astype(jnp.int32), axis=1))

def layer_norm(values, gain, bias):
    center = values - lax.optimization_barrier(jnp.mean(values, axis=1, keepdims=True))
    spread = lax.optimization_barrier(jnp.mean(center * center, axis=1, keepdims=True))
    return center * lax.rsqrt(spread + LN_EPS) * gain + bias

def reference(hidden_in, qkv_weight, stretch_len, out_weight, ln1_gain, ln1_bias, up_weight, down_weight, ln2_gain, ln2_bias, dec_query, kv_cache, piece_req, piece_used):
    inv_scale = 1.0 / math.sqrt(HD)
    qblock = min(512, BLK)
    span = qblock + 2 * REACH
    prefill_qkv = jnp.stack([jnp.dot(hidden_in, qkv_weight[:, part_index, :], preferred_element_type=jnp.float32).astype(jnp.bfloat16) for part_index in range(3)])
    all_rows = jnp.arange(PTOK, dtype=jnp.int32)
    segment = segment_ids(all_rows, stretch_len)
    padded = jnp.pad(prefill_qkv[1:], ((0, 0), (REACH, REACH), (0, 0)))
    padded_seg = jnp.pad(segment, (REACH, REACH), constant_values=-1)
    distance = jnp.arange(span, dtype=jnp.int32)[None, :] - REACH - jnp.arange(qblock, dtype=jnp.int32)[:, None]

    def prefill_block(block_index):
        first_row = (block_index * qblock).astype(jnp.int32)
        queries = lax.dynamic_slice_in_dim(prefill_qkv[0], first_row, qblock, 0).astype(jnp.float32).reshape(qblock, H, HD)
        both = lax.dynamic_slice_in_dim(padded, first_row, span, 1).astype(jnp.float32)
        key_rows = both[0].reshape(span, H, HD)
        value_rows = both[1].reshape(span, H, HD)
        key_seg = lax.dynamic_slice_in_dim(padded_seg, first_row, span, 0)
        query_seg = lax.dynamic_slice_in_dim(segment, first_row, qblock, 0)
        allowed = (key_seg[None, :] == query_seg[:, None]) & (jnp.abs(distance) <= REACH)
        scores = jnp.einsum('ihd,jhd->hij', queries, key_rows) * inv_scale
        scores = jnp.where(allowed[None], scores, NEG_FILL)
        row_max = lax.optimization_barrier(jnp.max(scores, axis=2, keepdims=True))
        weights = jnp.where(allowed[None], jnp.exp(scores - row_max), 0.0)
        totals = lax.optimization_barrier(jnp.sum(weights, axis=2))
        rounded = weights.astype(jnp.bfloat16).astype(jnp.float32)
        summed = jnp.einsum('hij,jhd->ihd', rounded, value_rows)
        return (summed / jnp.transpose(totals)[:, :, None]).astype(jnp.bfloat16).reshape(qblock, D)
    attention = lax.map(prefill_block, jnp.arange(PTOK // qblock, dtype=jnp.int32)).reshape(PTOK, D)
    projected = jnp.dot(attention, out_weight, preferred_element_type=jnp.float32)
    normed = layer_norm(hidden_in.astype(jnp.float32) + projected, ln1_gain, ln1_bias).astype(jnp.bfloat16)
    units = jax.nn.gelu(jnp.dot(normed, up_weight, preferred_element_type=jnp.float32), approximate=False).astype(jnp.bfloat16)
    ffn = jnp.dot(units, down_weight, preferred_element_type=jnp.float32)
    prefill_out = layer_norm(normed.astype(jnp.float32) + ffn, ln2_gain, ln2_bias).astype(jnp.bfloat16)

    def decode_group(group_index):
        first_req = (group_index * RQ_TOK).astype(jnp.int32)
        queries = lax.dynamic_slice_in_dim(dec_query, first_req, RQ_TOK, 0).astype(jnp.float32)
        owners = piece_req[group_index]
        filled = piece_used[group_index]
        key_rows = kv_cache[0, group_index].astype(jnp.float32).reshape(SLOTS, PLEN, H, HD)
        value_rows = kv_cache[1, group_index].astype(jnp.float32).reshape(SLOTS, PLEN, H, HD)
        chosen = queries[owners].reshape(SLOTS, H, HD)
        scores = jnp.einsum('phd,pthd->pht', chosen, key_rows) * inv_scale
        active = jnp.arange(PLEN, dtype=jnp.int32)[None, :] < filled[:, None]
        scores = jnp.where(active[:, None, :], scores, NEG_FILL)
        piece_max = lax.optimization_barrier(jnp.max(scores, axis=2))
        weights = jnp.where(active[:, None, :], jnp.exp(scores - piece_max[:, :, None]), 0.0)
        totals = lax.optimization_barrier(jnp.sum(weights, axis=2))
        partial_value = jnp.einsum('pht,pthd->phd', weights.astype(jnp.bfloat16).astype(jnp.float32), value_rows)
        member = (owners[None, :] == jnp.arange(RQ_TOK, dtype=jnp.int32)[:, None]) & (filled[None, :] > 0)
        highest = lax.optimization_barrier(jnp.max(jnp.where(member[:, :, None], piece_max[None], NEG_FILL), axis=1))
        factor = jnp.where(member[:, :, None], jnp.exp(piece_max[None] - highest[:, None, :]), 0.0)
        denom = lax.optimization_barrier(jnp.sum(factor * totals[None], axis=1))
        weighted = jnp.einsum('rph,phd->rhd', factor, partial_value)
        return (weighted / denom[:, :, None]).astype(jnp.bfloat16).reshape(RQ_TOK, D)
    dec_out = lax.map(decode_group, jnp.arange(N_TOK, dtype=jnp.int32)).reshape(REQ, D)
    return (prefill_out, dec_out)
```

```python
import functools
import math

import jax
import jax.numpy as jnp
from jax import lax
from jax.experimental import pallas as pl
from jax.experimental.pallas import tpu as pltpu
from jax.sharding import PartitionSpec as P

MESH = pl.DeviceIdType.MESH
F32 = jnp.float32
BF16 = jnp.bfloat16
D = 1024
NZ = 8
NK = 16
NX = 4
NY = 8
NT = NX * NY
NSEG = 48
NPIECE = 6
REACH = 256
NEG = -1e30
EPS = 1e-5


def rem(value, count):
    return lax.rem(value, count)


def layer_norm(values, gain, bias):
    center = values - jnp.mean(values, axis=1, keepdims=True)
    spread = jnp.mean(center * center, axis=1, keepdims=True)
    return center * lax.rsqrt(spread + EPS) * gain + bias


def gelu(v):
    return v * (0.5 + 0.5 * lax.erf(v * (1.0 / math.sqrt(2.0))))


def kernel(
    hid, wqkv, slen, wo, g1, b1, up, dn, g2, b2, dq, kvc, preq, pused,
    out, dec,
    xb, wob, upb, dnb, kvb, qb, wraw, wcat, ab, ar, atb, nb, rso, rsi, pxo, pxi, cache,
    dqf, dqs, dqb, po, pm, pz, gq, do_, ds_, dor, dsr,
    loc_sem,
    hzs, hzr, hss, hsr,
    wzs, wzr, wss, wsr,
    seeds_s, seeds_r, a1s, a1r, a2s, a2r, b1s, b1r, b2s, b2r,
    halo_s, halo_r,
    aas, aar,
    dqss, dqsr, dcs, dcr, dts, dtr,
    ns, nr, fs, fr,
):
    t = lax.axis_index("tok")
    kv = lax.axis_index("kv")
    z, c = kv // 2, rem(kv, 2)
    y, x = t // NX, rem(t, NX)
    sib = (t, 2 * z + (1 - c))

    def remote(src, dst, ss, rs, dev):
        return pltpu.make_async_remote_copy(
            src_ref=src, dst_ref=dst, send_sem=ss, recv_sem=rs,
            device_id=dev, device_id_type=MESH,
        )

    sent = []

    def start(src, dst, ss, rs, dev):
        copy = remote(src, dst, ss, rs, dev)
        copy.start()
        sent.append(copy)

    def arrived(dst, rs):
        remote(dst, dst, loc_sem.at[0], rs, sib).wait_recv()

    own_rows = pl.ds(pl.multiple_of(kv * 64, 64), 64)
    local = [
        pltpu.make_async_copy(hid, xb.at[own_rows], loc_sem.at[0]),
        pltpu.make_async_copy(wqkv, wraw, loc_sem.at[1]),
        pltpu.make_async_copy(wo, wob.at[own_rows], loc_sem.at[2]),
        pltpu.make_async_copy(up, upb.at[0], loc_sem.at[3]),
        pltpu.make_async_copy(dn, dnb.at[0], loc_sem.at[4]),
        pltpu.make_async_copy(kvc.at[:, 0], cache, loc_sem.at[5]),
    ]
    for copy in local:
        copy.start()

    barrier = pltpu.get_barrier_semaphore()
    peers = [(t, rem(kv + o, NK)) for o in range(1, NK)]
    peers += [(y * NX + rem(x + o, NX), kv) for o in range(1, NX)]
    yup, ydown = (rem(y + 1, NY) * NX + x, kv), (rem(y + NY - 1, NY) * NX + x, kv)
    peers += [yup, ydown]
    tnext, tprev = (rem(t + 1, NT), kv), (rem(t + NT - 1, NT), kv)
    peers += [tnext, tprev]
    for peer in peers:
        pl.semaphore_signal(barrier, inc=1, device_id=peer, device_id_type=MESH)
    pl.semaphore_wait(barrier, len(peers))

    zdev = [(t, 2 * rem(z + 1, NZ) + c), (t, 2 * rem(z + NZ - 1, NZ) + c)]

    def at_hop(d, k):
        return rem(z + NZ - k, NZ) if d == 0 else rem(z + k, NZ)

    def part(zz, core, h):
        return pl.ds(pl.multiple_of((2 * zz + core) * 64 + 32 * h, 32), 32)

    def idx(d, k, h):
        return (d * 4 + k - 1) * 2 + h

    def ring_send(buf, own, zs, zr, k, d, h):
        if k == 4 and h != d:
            return
        zz = at_hop(d, k - 1)
        src = own.at[pl.ds(32 * h, 32)] if k == 1 else buf.at[part(zz, c, h)]
        start(src, buf.at[part(zz, c, h)], zs.at[idx(d, k, h)], zr.at[idx(d, k, h)], zdev[d])

    def ring_first(buf, own, zs, zr, ss, sr):
        for h in range(2):
            for d in range(2):
                ring_send(buf, own, zs, zr, 1, d, h)
        start(own, buf.at[own_rows], ss.at[16], sr.at[16], sib)

    def ring_hop(buf, own, zs, zr, ss, sr, k):
        for h in range(2):
            for d in range(2):
                if k == 4 and h != d:
                    continue
                here = buf.at[part(at_hop(d, k), c, h)]
                arrived(here, zr.at[idx(d, k, h)])
                if k < 4:
                    ring_send(buf, own, zs, zr, k + 1, d, h)
                start(here, here, ss.at[idx(d, k, h)], sr.at[idx(d, k, h)], sib)

    def ring_relayed(buf, sr, k, d):
        for h in range(2):
            if k == 4 and h != d:
                continue
            arrived(buf.at[part(at_hop(d, k), 1 - c, h)], sr.at[idx(d, k, h)])

    hidden = (xb, hid, hzs, hzr, hss, hsr)
    outw = (wob, wo, wzs, wzr, wss, wsr)
    sib_rows = pl.ds(pl.multiple_of((2 * z + 1 - c) * 64, 64), 64)

    ring_first(*hidden)

    up_rows = pl.ds(pl.multiple_of(t * 32, 32), 32)

    def dn_block(xx, yy):
        return (
            pl.ds(pl.multiple_of(64 * xx + 16 * rem(yy, 4), 16), 16),
            pl.ds(pl.multiple_of(512 * (yy // 4), 512), 512),
        )

    dr, dcol = dn_block(x, y)
    for j in range(1, 4):
        dev = (t, rem(kv + NK - 4 * j, NK))
        start(up.at[up_rows, :], upb.at[j, up_rows, :], seeds_s.at[j - 1], seeds_r.at[j - 1], dev)
        start(dn.at[dr, dcol], dnb.at[j, dr, dcol], seeds_s.at[j + 2], seeds_r.at[j + 2], dev)

    qf = dq[...].astype(F32)
    for i in range(8):
        dqf[pl.ds(2 * i, 2), :] = qf[:, 128 * i : 128 * i + 128]
    dqs[...] = dqf[...].astype(BF16)
    dqb[kv] = dqs[...]

    def send_query(o, carry):
        dev = rem(kv + o, NK)
        remote(dqs, dqb.at[kv], dqss.at[o - 1], dqsr.at[kv], (t, dev)).start()
        return carry

    lax.fori_loop(1, NK, send_query, 0)

    first = t * D
    lane = lax.broadcasted_iota(jnp.int32, (1, 128), 1)
    ends = jnp.zeros((1, 128), jnp.int32)

    def add_len(i, ends):
        return ends + jnp.where(lane >= i, slen[i], 0)

    ends = (lax.fori_loop(0, NSEG, add_len, ends) - first).astype(F32)
    floor = (-first).astype(F32)

    local[1].wait()
    zero = jnp.zeros((D, 64), BF16)
    wcat[:, 0:128] = jnp.concatenate([wraw[:, 0, :], zero], axis=1)
    wcat[:, 128:256] = jnp.concatenate([wraw[:, 1, :], wraw[:, 2, :]], axis=1)

    def project(zz):
        rows = pl.ds(pl.multiple_of(zz * 128, 128), 128)
        res = jnp.dot(xb[rows, :], wcat[...], preferred_element_type=F32).astype(BF16)
        qb[rows, :] = res[:, 0:128] * 0.125
        kvb[pl.ds(pl.multiple_of(zz * 128 + REACH, 128), 128), :] = res[:, 128:256]

    ring_hop(*hidden, 1)
    local[0].wait()
    arrived(xb.at[sib_rows], hsr.at[16])
    project(z)

    def xdev(o):
        return (y * NX + rem(x + o, NX), kv)

    ydev = [yup, ydown]

    def y_at(d, k):
        return rem(y + NY - k, NY) if d == 0 else rem(y + k, NY)

    def a2_block(yy, half=None):
        if half is None:
            return upb.at[pl.ds(1, 3), pl.ds(pl.multiple_of(yy * 128, 128), 128), :]
        return upb.at[pl.ds(1, 3), pl.ds(pl.multiple_of(yy * 128 + 64 * half, 64), 64), :]

    def b1_block(yy, half=None):
        r, cc = dn_block(x, yy)
        if half is not None:
            cc = pl.ds(pl.multiple_of(512 * (yy // 4) + 256 * half, 256), 256)
        return dnb.at[pl.ds(1, 3), r, cc]

    def y_send(block, ss, sr, k):
        for d in range(2):
            ref = block(y_at(d, k - 1), d if k == 4 else None)
            start(ref, ref, ss.at[d * 4 + k - 1], sr.at[d * 4 + k - 1], ydev[d])

    def y_wait(block, sr, k):
        for d in range(2):
            arrived(block(y_at(d, k), d if k == 4 else None), sr.at[d * 4 + k - 1])

    for j in range(1, 4):
        arrived(upb.at[j, up_rows, :], seeds_r.at[j - 1])
        arrived(dnb.at[j, dr, dcol], seeds_r.at[j + 2])
    seed = upb.at[pl.ds(1, 3), up_rows, :]
    for o in range(1, NX):
        start(seed, seed, a1s.at[o - 1], a1r.at[o - 1], xdev(o))
    y_send(b1_block, b1s, b1r, 1)

    ring_hop(*hidden, 2)
    for d in range(2):
        ring_relayed(xb, hsr, 1, d)
        project(at_hop(d, 1))

    for o in range(1, NX):
        rows = pl.ds(pl.multiple_of((y * NX + rem(x + NX - o, NX)) * 32, 32), 32)
        arrived(upb.at[pl.ds(1, 3), rows, :], a1r.at[o - 1])
    y_send(a2_block, a2s, a2r, 1)
    y_wait(b1_block, b1r, 1)
    y_send(b1_block, b1s, b1r, 2)

    ring_hop(*hidden, 3)
    for d in range(2):
        ring_relayed(xb, hsr, 2, d)
        project(at_hop(d, 2))
    y_wait(b1_block, b1r, 2)
    y_send(b1_block, b1s, b1r, 3)

    def got_query(o, carry):
        src = rem(kv + o, NK)
        arrived(dqb.at[src], dqsr.at[src])
        return carry

    lax.fori_loop(1, NK, got_query, 0)
    row48 = lax.broadcasted_iota(jnp.int32, (48, 1), 0)
    target = 2 * rem(row48, 8)
    for p in range(NPIECE):
        n = preq[0, p]
        target = target + jnp.where(row48 // 8 == p, 16 * (n // 2) + rem(n, 2), 0)
    col256 = lax.broadcasted_iota(jnp.int32, (48, 256), 1)
    select = (col256 == target).astype(F32).astype(BF16)
    gq[...] = jnp.dot(select, dqb[...].reshape(256, 128), preferred_element_type=F32)
    local[5].wait()
    head16 = lax.broadcasted_iota(jnp.int32, (16, 128), 0)
    lane16 = lax.broadcasted_iota(jnp.int32, (16, 128), 1)
    masks = [head16 == 2 * i + lane16 // 64 for i in range(8)]

    def piece(p, carry):
        g = gq[pl.ds(pl.multiple_of(8 * p, 8), 8), :]
        qbd = jnp.concatenate(
            [jnp.where(masks[i], g[i : i + 1, :], 0.0) for i in range(8)], axis=1
        ).astype(BF16)
        u = lax.dot_general(
            qbd, cache[0, p], (((1,), (1,)), ((), ())), preferred_element_type=F32
        ) * 0.125
        live = lane16 < pused[0, p]
        u = jnp.where(live, u, NEG)
        m = jnp.max(u, axis=1, keepdims=True)
        e = jnp.where(live, jnp.exp(u - m), 0.0)
        s = jnp.sum(e, axis=1, keepdims=True)
        o = jnp.dot(e.astype(BF16), cache[1, p], preferred_element_type=F32)
        for i in range(8):
            po[p, i : i + 1, :] = jnp.sum(
                jnp.where(masks[i], o[:, 128 * i : 128 * i + 128], 0.0), axis=0, keepdims=True
            )
            pm[p, i : i + 1, :] = jnp.sum(jnp.where(masks[i], m, 0.0), axis=0, keepdims=True)
            pz[p, i : i + 1, :] = jnp.sum(jnp.where(masks[i], s, 0.0), axis=0, keepdims=True)
        return carry

    lax.fori_loop(0, NPIECE, piece, 0)
    lane8 = rem(lax.broadcasted_iota(jnp.int32, (8, 128), 1), 64)

    def combine(d, carry):
        values, stats = [], jnp.zeros((8, 128), F32)
        for r in range(2):
            mine = [(preq[0, p] == 2 * d + r) & (pused[0, p] > 0) for p in range(NPIECE)]
            top = jnp.full((8, 128), NEG, F32)
            for p in range(NPIECE):
                top = jnp.maximum(top, jnp.where(mine[p], pm[p], NEG))
            total = jnp.zeros((8, 128), F32)
            value = jnp.zeros((8, 128), F32)
            for p in range(NPIECE):
                factor = jnp.where(mine[p], jnp.exp(pm[p] - top), 0.0)
                total = total + factor * pz[p]
                value = value + factor * po[p]
            values.append(value)
            stats = jnp.where(lane8 == 2 * r, top, jnp.where(lane8 == 2 * r + 1, total, stats))
        do_[d] = jnp.concatenate(values, axis=0).astype(BF16)
        ds_[d] = stats
        return carry

    lax.fori_loop(0, NK, combine, 0)
    dor[kv] = do_[kv]
    dsr[kv] = ds_[kv]

    ring_hop(*hidden, 4)
    for d in range(2):
        ring_relayed(xb, hsr, 3, d)
        project(at_hop(d, 3))
    for d in range(2):
        ring_relayed(xb, hsr, 4, d)
    project(at_hop(0, 4))

    low, high = pl.ds(REACH, REACH), pl.ds(D, REACH)
    start(kvb.at[low], kvb.at[pl.ds(D + REACH, REACH)], halo_s.at[0], halo_r.at[0], tprev)
    start(kvb.at[high], kvb.at[pl.ds(0, REACH)], halo_s.at[1], halo_r.at[1], tnext)

    local[2].wait()
    ring_first(*outw)

    y_wait(a2_block, a2r, 1)
    y_send(a2_block, a2s, a2r, 2)
    y_wait(b1_block, b1r, 3)
    y_send(b1_block, b1s, b1r, 4)

    def attend(b):
        r0 = 256 * b
        q = qb[pl.ds(r0, 256), :]
        keys = kvb[pl.ds(r0, 768), :]
        s = lax.dot_general(q, keys, (((1,), (1,)), ((), ())), preferred_element_type=F32)
        row = (r0 + lax.broadcasted_iota(jnp.int32, (256, 1), 0)).astype(F32)
        begin = jnp.max(jnp.where(ends <= row, ends, floor), axis=1, keepdims=True)
        end = jnp.min(jnp.where(ends > row, ends, 1e9), axis=1, keepdims=True)
        lo = jnp.maximum(begin, row - REACH)
        hi = jnp.minimum(end - 1.0, row + REACH)
        kid = (r0 - REACH + lax.broadcasted_iota(jnp.int32, (1, 768), 1)).astype(F32)
        s = jnp.where((kid >= lo) & (kid <= hi), s, NEG)
        m = jnp.max(s, axis=1, keepdims=True)
        w = jnp.exp(s - m)
        total = jnp.sum(w, axis=1, keepdims=True)
        o = jnp.dot(w.astype(BF16), keys, preferred_element_type=F32) / total
        o = o.reshape(4, 2, 32, 128)
        turned = pltpu.roll(o[:, 0].reshape(128, 128), 64, 1)
        lanes = lax.broadcasted_iota(jnp.int32, (128, 128), 1)
        packed = jnp.where(lanes < 64, turned, o[:, 1].reshape(128, 128)).astype(BF16)
        ab[pl.ds(4 * b, 4)] = packed.reshape(4, 32, 128)

        def send_heads(i, carry):
            d = 4 * b + i

            @pl.when(d != kv)
            def _():
                remote(ab.at[d], ar.at[kv], aas.at[d], aar.at[kv], (t, d)).start()

            @pl.when(d == kv)
            def _():
                ar[kv] = ab[d]

            return carry

        lax.fori_loop(0, 4, send_heads, 0)

    attend(1)
    attend(2)
    ring_hop(*outw, 1)
    arrived(kvb.at[pl.ds(D + REACH, REACH)], halo_r.at[0])
    arrived(kvb.at[pl.ds(0, REACH)], halo_r.at[1])
    attend(0)
    attend(3)
    ring_hop(*outw, 2)

    def send_partial(o, carry):
        dev = rem(kv + o, NK)
        remote(do_.at[dev], dor.at[kv], dcs.at[dev], dcr.at[kv], (t, dev)).start()
        remote(ds_.at[dev], dsr.at[kv], dts.at[dev], dtr.at[kv], (t, dev)).start()
        return carry

    lax.fori_loop(1, NK, send_partial, 0)

    y_wait(a2_block, a2r, 2)
    y_send(a2_block, a2s, a2r, 3)
    y_wait(b1_block, b1r, 4)
    slab = dnb.at[pl.ds(1, 3), pl.ds(pl.multiple_of(64 * x, 64), 64), :]
    for o in range(1, NX):
        start(slab, slab, b2s.at[o - 1], b2r.at[o - 1], xdev(o))

    ring_hop(*outw, 3)
    ring_hop(*outw, 4)
    y_wait(a2_block, a2r, 3)
    y_send(a2_block, a2s, a2r, 4)

    def got_heads(o, carry):
        src = rem(kv + o, NK)
        arrived(ar.at[src], aar.at[src])
        return carry

    lax.fori_loop(1, NK, got_heads, 0)
    lanes32 = lax.broadcasted_iota(jnp.int32, (32, 128), 1)
    for j in range(8):
        m0, m1 = ar[2 * j].astype(F32), ar[2 * j + 1].astype(F32)
        cols = pl.ds(128 * j, 128)
        atb[pl.ds(0, 32), cols] = jnp.where(lanes32 < 64, m0, pltpu.roll(m1, 64, 1)).astype(BF16)
        atb[pl.ds(32, 32), cols] = jnp.where(lanes32 < 64, pltpu.roll(m0, 64, 1), m1).astype(BF16)

    arrived(wob.at[sib_rows], wsr.at[16])
    for k in range(1, 5):
        for d in range(2):
            ring_relayed(wob, wsr, k, d)
    projected = jnp.dot(atb[...], wob[...], preferred_element_type=F32)
    own = xb[own_rows, :].astype(F32)
    normed = layer_norm(own + projected, g1[...], b1[...]).astype(BF16)

    gi = rem(kv, 4)
    odd = rem(z, 2)
    pair = (t, 2 * (z + 1 - 2 * odd) + c)
    nb[pl.ds(pl.multiple_of(gi * 64, 64), 64), :] = normed

    def nrows(zz, core, h):
        return pl.ds(pl.multiple_of((2 * zz + core) * 64 + 32 * h, 32), 32)

    mine = nb.at[pl.ds(pl.multiple_of(gi * 64, 64), 64)]
    for h in range(2):
        ref = nb.at[nrows(odd, c, h)]
        start(ref, ref, ns.at[h], nr.at[h], pair)
    start(mine, mine, ns.at[2], nr.at[2], sib)

    local[3].wait()
    local[4].wait()
    y_wait(a2_block, a2r, 4)
    for o in range(1, NX):
        rows = pl.ds(pl.multiple_of(64 * rem(x + NX - o, NX), 64), 64)
        arrived(dnb.at[pl.ds(1, 3), rows, :], b2r.at[o - 1])

    def ffn(zz):
        rows = nb[pl.ds(pl.multiple_of(zz * 128, 128), 128), :]
        acc = jnp.zeros((128, D), F32)
        for j in range(4):
            units = gelu(jnp.dot(rows, upb[j], preferred_element_type=F32)).astype(BF16)
            acc = acc + jnp.dot(units, dnb[j], preferred_element_type=F32)
        return acc

    arrived(nb.at[pl.ds(pl.multiple_of((2 * odd + 1 - c) * 64, 64), 64)], nr.at[2])
    for h in range(2):
        ref = nb.at[nrows(1 - odd, c, h)]
        arrived(ref, nr.at[h])
        start(ref, ref, ns.at[3 + h], nr.at[3 + h], sib)
    acc = ffn(odd)

    def split(acc):
        low, high = acc[0:64], acc[64:128]
        first = c == 0
        return jnp.where(first, low, high), jnp.where(first, high, low)

    kept, other = split(acc)
    rso[0] = other.astype(BF16)
    start(rso.at[0], rsi.at[0], fs.at[0], fr.at[0], sib)
    for h in range(2):
        arrived(nb.at[nrows(1 - odd, 1 - c, h)], nr.at[3 + h])
    ahead, other = split(ffn(1 - odd))
    rso[1] = other.astype(BF16)
    start(rso.at[1], rsi.at[1], fs.at[1], fr.at[1], sib)
    arrived(rsi.at[1], fr.at[1])
    pxo[...] = (ahead + rsi[1].astype(F32)).astype(BF16)
    start(pxo, pxi, fs.at[2], fr.at[2], pair)

    def got_partial(o, carry):
        src = rem(kv + o, NK)
        arrived(dor.at[src], dcr.at[src])
        arrived(dsr.at[src], dtr.at[src])
        return carry

    lax.fori_loop(1, NK, got_partial, 0)
    stats = dsr[...]
    lane3 = lax.broadcasted_iota(jnp.int32, (NK, 8, 128), 2)

    def spread(at):
        a = jnp.sum(jnp.where(lane3 == at, stats, 0.0), axis=2, keepdims=True)
        b = jnp.sum(jnp.where(lane3 == at + 64, stats, 0.0), axis=2, keepdims=True)
        return jnp.where(lane3 < 64, a, b)

    done = []
    for r in range(2):
        top, total = spread(2 * r), spread(2 * r + 1)
        value = dor[:, 8 * r : 8 * r + 8, :].astype(F32)
        factor = jnp.exp(top - jnp.max(top, axis=0, keepdims=True))
        value = jnp.sum(factor * value, axis=0) / jnp.sum(factor * total, axis=0)
        done.append(jnp.concatenate([value[i : i + 1, :] for i in range(8)], axis=1))
    dec[...] = jnp.concatenate(done, axis=0).astype(BF16)

    arrived(rsi.at[0], fr.at[0])
    kept = kept + rsi[0].astype(F32) + nb[pl.ds(pl.multiple_of(gi * 64, 64), 64), :].astype(F32)
    arrived(pxi, fr.at[2])
    out[...] = layer_norm(kept + pxi[...].astype(F32), g2[...], b2[...]).astype(BF16)

    for copy in sent:
        copy.wait_send()

    def sent_small(o, carry):
        dev = rem(kv + o, NK)
        remote(dqs, dqb.at[kv], dqss.at[o - 1], dqsr.at[kv], (t, dev)).wait_send()
        remote(ab.at[dev], ar.at[kv], aas.at[dev], aar.at[kv], (t, dev)).wait_send()
        remote(do_.at[dev], dor.at[kv], dcs.at[dev], dcr.at[kv], (t, dev)).wait_send()
        remote(ds_.at[dev], dsr.at[kv], dts.at[dev], dtr.at[kv], (t, dev)).wait_send()
        return carry

    lax.fori_loop(1, NK, sent_small, 0)


def body(hid, wqkv, slen, wo, g1, b1, up, dn, g2, b2, dq, kvc, preq, pused):
    vm = pl.BlockSpec(memory_space=pltpu.VMEM)
    hbm = pl.BlockSpec(memory_space=pl.ANY)
    sm = pl.BlockSpec(memory_space=pltpu.SMEM)
    dma = pltpu.SemaphoreType.DMA
    V = pltpu.VMEM
    return pl.pallas_call(
        kernel,
        out_shape=(
            jax.ShapeDtypeStruct((64, D), BF16),
            jax.ShapeDtypeStruct((2, D), BF16),
        ),
        in_specs=[hbm, hbm, sm, hbm, vm, vm, hbm, hbm, vm, vm, vm, hbm, sm, sm],
        out_specs=(vm, vm),
        scratch_shapes=[
            V((D, D), BF16), V((D, D), BF16), V((4, D, 256), BF16), V((4, 256, D), BF16),
            V((D + 2 * REACH, 128), BF16), V((D, 128), BF16), V((D, 3, 64), BF16), V((D, 256), BF16),
            V((NK, 32, 128), BF16), V((NK, 32, 128), BF16), V((64, D), BF16), V((256, D), BF16),
            V((2, 64, D), BF16), V((2, 64, D), BF16), V((64, D), BF16), V((64, D), BF16),
            V((2, NPIECE, 128, D), BF16),
            V((16, 128), F32), V((16, 128), BF16), V((NK, 16, 128), BF16),
            V((NPIECE, 8, 128), F32), V((NPIECE, 8, 128), F32), V((NPIECE, 8, 128), F32), V((48, 128), F32),
            V((NK, 16, 128), BF16), V((NK, 8, 128), F32), V((NK, 16, 128), BF16), V((NK, 8, 128), F32),
            dma((6,)),
            dma((16,)), dma((16,)), dma((17,)), dma((17,)),
            dma((16,)), dma((16,)), dma((17,)), dma((17,)),
            dma((6,)), dma((6,)), dma((3,)), dma((3,)), dma((8,)), dma((8,)),
            dma((8,)), dma((8,)), dma((3,)), dma((3,)),
            dma((2,)), dma((2,)),
            dma((NK,)), dma((NK,)),
            dma((NK,)), dma((NK,)), dma((NK,)), dma((NK,)), dma((NK,)), dma((NK,)),
            dma((5,)), dma((5,)), dma((3,)), dma((3,)),
        ],
        compiler_params=pltpu.CompilerParams(
            collective_id=0, has_side_effects=True, vmem_limit_bytes=48 * 1024 * 1024
        ),
    )(hid, wqkv, slen, wo, g1.reshape(1, D), b1.reshape(1, D), up, dn, g2.reshape(1, D), b2.reshape(1, D), dq, kvc, preq, pused)


def solution(mesh):
    rows = P(("tok", "kv"), None)
    placed = (
        rows, P(None, None, "kv"), P(), P("kv", None), P(), P(), P(None, "kv"), P("kv", None),
        P(), P(), rows, P(None, "tok", "kv", None, None), P("tok", "kv"), P("tok", "kv"),
    )
    return jax.shard_map(
        body, mesh=mesh, in_specs=placed, out_specs=(rows, rows), check_vma=False
    )
```

```python
import functools
import math

import jax
import jax.numpy as jnp
from jax import lax
from jax.experimental import pallas as pl
from jax.experimental.pallas import tpu as pltpu
from jax.sharding import PartitionSpec as P

MESH = pl.DeviceIdType.MESH
F32 = jnp.float32
BF16 = jnp.bfloat16
D = 1024
NZ = 8
NK = 16
NX = 4
NY = 8
NT = NX * NY
NSEG = 48
NPIECE = 6
REACH = 256
NEG = -1e30
EPS = 1e-5


def rem(value, count):
    return lax.rem(value, count)


def layer_norm(values, gain, bias):
    center = values - jnp.mean(values, axis=1, keepdims=True)
    spread = jnp.mean(center * center, axis=1, keepdims=True)
    return center * lax.rsqrt(spread + EPS) * gain + bias


def gelu(v):
    return v * (0.5 + 0.5 * lax.erf(v * (1.0 / math.sqrt(2.0))))


def kernel(
    hid, wqkv, slen_in, wo, g1_in, b1_in, up, dn, g2_in, b2_in, dq_in, kvc, preq_in, pused_in,
    out, dec,
    g1, b1, g2, b2, dq, slen, preq, pused,
    xb, wob, upb, dnb, kvb, qb, wcat, wtr, ab, ar, atb, nb, rso, rsi, pxo, pxi, qso, qsi, qxo, qxi, cache,
    dqf, dqs, dqb, po, pm, pz, gq, do_, ds_, dor, dsr,
    loc_sem,
    hzs, hzr, hss, hsr,
    seeds_s, seeds_r, a1s, a1r, a2s, a2r, b1s, b1r, b2s, b2r, w1s, w1r, w2s, w2r, ps, pr,
    halo_s, halo_r,
    aas, aar,
    dqss, dqsr, dcs, dcr, dts, dtr,
    ns, nr, fs, fr,
):
    t = lax.axis_index("tok")
    kv = lax.axis_index("kv")
    z, c = kv // 2, rem(kv, 2)
    y, x = t // NX, rem(t, NX)
    sib = (t, 2 * z + (1 - c))

    def remote(src, dst, ss, rs, dev):
        return pltpu.make_async_remote_copy(
            src_ref=src, dst_ref=dst, send_sem=ss, recv_sem=rs,
            device_id=dev, device_id_type=MESH,
        )

    sent = []

    def start(src, dst, ss, rs, dev):
        copy = remote(src, dst, ss, rs, dev)
        copy.start()
        sent.append(copy)

    def arrived(dst, rs):
        remote(dst, dst, loc_sem.at[0], rs, sib).wait_recv()

    own_rows = pl.ds(pl.multiple_of(kv * 64, 64), 64)
    local = [
        pltpu.make_async_copy(hid, xb.at[own_rows], loc_sem.at[0]),
        pltpu.make_async_copy(wqkv.at[0], wcat.at[pl.ds(0, 64)], loc_sem.at[1]),
        pltpu.make_async_copy(wo, wob.at[0], loc_sem.at[2]),
        pltpu.make_async_copy(up, upb.at[0], loc_sem.at[3]),
        pltpu.make_async_copy(dn, dnb.at[0], loc_sem.at[4]),
        pltpu.make_async_copy(kvc.at[:, 0], cache, loc_sem.at[5]),
        pltpu.make_async_copy(wqkv.at[1], wcat.at[pl.ds(128, 64)], loc_sem.at[6]),
        pltpu.make_async_copy(wqkv.at[2], wcat.at[pl.ds(192, 64)], loc_sem.at[7]),
        pltpu.make_async_copy(dq_in, dq, loc_sem.at[8]),
        pltpu.make_async_copy(slen_in, slen, loc_sem.at[9]),
        pltpu.make_async_copy(preq_in, preq, loc_sem.at[10]),
        pltpu.make_async_copy(pused_in, pused, loc_sem.at[11]),
        pltpu.make_async_copy(g1_in, g1, loc_sem.at[12]),
        pltpu.make_async_copy(b1_in, b1, loc_sem.at[13]),
        pltpu.make_async_copy(g2_in, g2, loc_sem.at[14]),
        pltpu.make_async_copy(b2_in, b2, loc_sem.at[15]),
    ]

    barrier = pltpu.get_barrier_semaphore()
    peers = [(t, rem(kv + o, NK)) for o in range(1, NK)]
    peers += [(y * NX + rem(x + o, NX), kv) for o in range(1, NX)]
    yup, ydown = (rem(y + 1, NY) * NX + x, kv), (rem(y + NY - 1, NY) * NX + x, kv)
    peers += [yup, ydown]
    tnext, tprev = (rem(t + 1, NT), kv), (rem(t + NT - 1, NT), kv)
    peers += [tnext, tprev]
    for peer in peers:
        pl.semaphore_signal(barrier, inc=1, device_id=peer, device_id_type=MESH)
    for i in (0, 8, 9):
        local[i].start()
    pl.semaphore_wait(barrier, len(peers))

    zdev = [(t, 2 * rem(z + 1, NZ) + c), (t, 2 * rem(z + NZ - 1, NZ) + c)]

    def at_hop(d, k):
        return rem(z + NZ - k, NZ) if d == 0 else rem(z + k, NZ)

    def part(zz, core, h):
        return pl.ds(pl.multiple_of((2 * zz + core) * 64 + 32 * h, 32), 32)

    def idx(d, k, h):
        return (d * 4 + k - 1) * 2 + h

    def ring_send(buf, own, zs, zr, k, d, h):
        if k == 4 and h != d:
            return
        zz = at_hop(d, k - 1)
        src = own.at[pl.ds(32 * h, 32)] if k == 1 else buf.at[part(zz, c, h)]
        start(src, buf.at[part(zz, c, h)], zs.at[idx(d, k, h)], zr.at[idx(d, k, h)], zdev[d])

    def ring_first(buf, own, zs, zr, ss, sr):
        for h in range(2):
            for d in range(2):
                ring_send(buf, own, zs, zr, 1, d, h)
        start(own, buf.at[own_rows], ss.at[16], sr.at[16], sib)

    def ring_hop(buf, own, zs, zr, ss, sr, k):
        for h in range(2):
            for d in range(2):
                if k == 4 and h != d:
                    continue
                here = buf.at[part(at_hop(d, k), c, h)]
                arrived(here, zr.at[idx(d, k, h)])
                if k < 4:
                    ring_send(buf, own, zs, zr, k + 1, d, h)
                start(here, here, ss.at[idx(d, k, h)], sr.at[idx(d, k, h)], sib)

    def ring_relayed(buf, sr, k, d):
        for h in range(2):
            if k == 4 and h != d:
                continue
            arrived(buf.at[part(at_hop(d, k), 1 - c, h)], sr.at[idx(d, k, h)])

    hidden = (xb, hid, hzs, hzr, hss, hsr)
    sib_rows = pl.ds(pl.multiple_of((2 * z + 1 - c) * 64, 64), 64)

    ring_first(*hidden)

    up_rows = pl.ds(pl.multiple_of(t * 32, 32), 32)

    def dn_block(xx, yy, half=None):
        if half is None:
            cols = pl.ds(pl.multiple_of(512 * (yy // 4), 512), 512)
        else:
            cols = pl.ds(pl.multiple_of(512 * (yy // 4) + 256 * half, 256), 256)
        return pl.ds(pl.multiple_of(64 * xx + 16 * rem(yy, 4), 16), 16), cols

    def wo_block(xx, yy):
        return (
            pl.ds(pl.multiple_of(16 * rem(yy, 4), 16), 16),
            pl.ds(pl.multiple_of(256 * xx + 128 * (yy // 4), 128), 128),
        )

    for i in (1, 6, 7, 10, 11, 5, 2, 3, 4, 12, 13, 14, 15):
        local[i].start()

    dr, dcol = dn_block(x, y)
    wr, wcol = wo_block(x, y)
    for j in range(1, 4):
        dev = (t, rem(kv + NK - 4 * j, NK))
        start(wo.at[wr, wcol], wob.at[j, wr, wcol], seeds_s.at[j + 5], seeds_r.at[j + 5], dev)
        start(up.at[up_rows, :], upb.at[j, up_rows, :], seeds_s.at[j - 1], seeds_r.at[j - 1], dev)
        start(dn.at[dr, dcol], dnb.at[j, dr, dcol], seeds_s.at[j + 2], seeds_r.at[j + 2], dev)

    local[8].wait()
    qf = dq[...].astype(F32)
    for i in range(8):
        dqf[pl.ds(2 * i, 2), :] = qf[:, 128 * i : 128 * i + 128]
    dqs[...] = dqf[...].astype(BF16)
    dqb[kv] = dqs[...]

    def send_query(o, carry):
        dev = rem(kv + o, NK)
        remote(dqs, dqb.at[kv], dqss.at[o - 1], dqsr.at[kv], (t, dev)).start()
        return carry

    lax.fori_loop(1, NK, send_query, 0)

    local[9].wait()
    first = t * D
    lane = lax.broadcasted_iota(jnp.int32, (1, 128), 1)
    ends = jnp.zeros((1, 128), jnp.int32)

    def add_len(i, ends):
        return ends + jnp.where(lane >= i, slen[i], 0)

    ends = (lax.fori_loop(0, NSEG, add_len, ends) - first).astype(F32)
    floor = (-first).astype(F32)

    wcat[pl.ds(64, 64), :] = jnp.zeros((64, D), BF16)
    for i in (1, 6, 7):
        local[i].wait()

    for i in range(4):
        rows = pl.ds(256 * i, 256)
        wtr[rows, :] = wcat[:, rows].astype(F32).T.astype(BF16)

    def project(zz):
        rows = pl.ds(pl.multiple_of(zz * 128, 128), 128)
        res = jnp.dot(xb[rows, :], wtr[...], preferred_element_type=F32).astype(BF16)
        qb[rows, :] = res[:, 0:128] * 0.125
        kvb[pl.ds(pl.multiple_of(zz * 128 + REACH, 128), 128), :] = res[:, 128:256]

    def project_pair(k):
        def one(d, carry):
            project(jnp.where(d == 0, rem(z + NZ - k, NZ), rem(z + k, NZ)))
            return carry

        lax.fori_loop(0, 2, one, 0)

    ring_hop(*hidden, 1)

    slots = pl.ds(1, 3)
    xdev = [(y * NX + rem(x + 1, NX), kv), (y * NX + rem(x + NX - 1, NX), kv)]
    ydev = [yup, ydown]

    def y_at(d, k):
        return rem(y + NY - k, NY) if d == 0 else rem(y + k, NY)

    def x_at(d, k):
        return rem(x + NX - k, NX) if d == 0 else rem(x + k, NX)

    def a2_block(yy, half):
        if half is None:
            return upb.at[slots, pl.ds(pl.multiple_of(yy * 128, 128), 128), :]
        return upb.at[slots, pl.ds(pl.multiple_of(yy * 128 + 64 * half, 64), 64), :]

    def b1_block(yy, half):
        r, cc = dn_block(x, yy, half)
        return dnb.at[slots, r, cc]

    def w1_block(yy, half):
        r, cc = wo_block(x, yy)
        return wob.at[slots, r, cc]

    def b2_block(xx, half):
        if half is None:
            return dnb.at[slots, pl.ds(pl.multiple_of(64 * xx, 64), 64), :]
        return dnb.at[slots, pl.ds(pl.multiple_of(64 * xx + 32 * half, 32), 32), :]

    def w2_block(xx, half):
        cols = pl.ds(pl.multiple_of(256 * xx, 256), 256)
        if half is None:
            return wob.at[slots, :, cols]
        return wob.at[slots, pl.ds(32 * half, 32), cols]

    def hop_send(block, at, devs, ss, sr, k, hops, whole=False):
        for d in range(2):
            if whole and k == hops and d == 1:
                continue
            ref = block(at(d, k - 1), d if k == hops and not whole else None)
            start(ref, ref, ss.at[d * hops + k - 1], sr.at[d * hops + k - 1], devs[d])

    def hop_wait(block, at, sr, k, hops, whole=False):
        for d in range(2):
            if whole and k == hops and d == 1:
                continue
            arrived(block(at(d, k), d if k == hops and not whole else None), sr.at[d * hops + k - 1])

    def a2_send(k):
        hop_send(a2_block, y_at, ydev, a2s, a2r, k, 4)

    def a2_wait(k):
        hop_wait(a2_block, y_at, a2r, k, 4)

    def b1_send(k):
        hop_send(w1_block, y_at, ydev, w1s, w1r, k, 4, True)
        hop_send(b1_block, y_at, ydev, b1s, b1r, k, 4)

    def b1_wait(k):
        hop_wait(w1_block, y_at, w1r, k, 4, True)
        hop_wait(b1_block, y_at, b1r, k, 4)

    for j in range(1, 4):
        arrived(wob.at[j, wr, wcol], seeds_r.at[j + 5])
        arrived(upb.at[j, up_rows, :], seeds_r.at[j - 1])
        arrived(dnb.at[j, dr, dcol], seeds_r.at[j + 2])
    seed = upb.at[slots, up_rows, :]
    for o in range(1, NX):
        start(seed, seed, a1s.at[o - 1], a1r.at[o - 1], (y * NX + rem(x + o, NX), kv))
    b1_send(1)
    local[0].wait()
    arrived(xb.at[sib_rows], hsr.at[16])
    project(z)

    ring_hop(*hidden, 2)
    for o in range(1, NX):
        rows = pl.ds(pl.multiple_of((y * NX + rem(x + NX - o, NX)) * 32, 32), 32)
        arrived(upb.at[slots, rows, :], a1r.at[o - 1])
    a2_send(1)
    b1_wait(1)
    b1_send(2)
    for d in range(2):
        ring_relayed(xb, hsr, 1, d)
    project_pair(1)

    def got_query(o, carry):
        src = rem(kv + o, NK)
        arrived(dqb.at[src], dqsr.at[src])
        return carry

    lax.fori_loop(1, NK, got_query, 0)
    local[10].wait()
    local[11].wait()
    row48 = lax.broadcasted_iota(jnp.int32, (48, 1), 0)
    target = 2 * rem(row48, 8)
    for p in range(NPIECE):
        n = preq[0, p]
        target = target + jnp.where(row48 // 8 == p, 16 * (n // 2) + rem(n, 2), 0)
    col256 = lax.broadcasted_iota(jnp.int32, (48, 256), 1)
    select = (col256 == target).astype(F32).astype(BF16)
    gq[...] = jnp.dot(select, dqb[...].reshape(256, 128), preferred_element_type=F32)
    local[5].wait()
    head16 = lax.broadcasted_iota(jnp.int32, (16, 128), 0)
    lane16 = lax.broadcasted_iota(jnp.int32, (16, 128), 1)
    masks = [head16 == 2 * i + lane16 // 64 for i in range(8)]

    def piece(p, carry):
        g = gq[pl.ds(pl.multiple_of(8 * p, 8), 8), :]
        qbd = jnp.concatenate(
            [jnp.where(masks[i], g[i : i + 1, :], 0.0) for i in range(8)], axis=1
        ).astype(BF16)
        u = lax.dot_general(
            qbd, cache[0, p], (((1,), (1,)), ((), ())), preferred_element_type=F32
        ) * 0.125
        live = lane16 < pused[0, p]
        u = jnp.where(live, u, NEG)
        m = jnp.max(u, axis=1, keepdims=True)
        e = jnp.where(live, jnp.exp(u - m), 0.0)
        s = jnp.sum(e, axis=1, keepdims=True)
        o = jnp.dot(e.astype(BF16), cache[1, p], preferred_element_type=F32)
        for i in range(8):
            po[p, i : i + 1, :] = jnp.sum(
                jnp.where(masks[i], o[:, 128 * i : 128 * i + 128], 0.0), axis=0, keepdims=True
            )
            pm[p, i : i + 1, :] = jnp.sum(jnp.where(masks[i], m, 0.0), axis=0, keepdims=True)
            pz[p, i : i + 1, :] = jnp.sum(jnp.where(masks[i], s, 0.0), axis=0, keepdims=True)
        return carry

    lax.fori_loop(0, NPIECE, piece, 0)

    ring_hop(*hidden, 3)
    b1_wait(2)
    b1_send(3)
    for d in range(2):
        ring_relayed(xb, hsr, 2, d)
    project_pair(2)
    lane8 = rem(lax.broadcasted_iota(jnp.int32, (8, 128), 1), 64)

    def combine(d, carry):
        values, stats = [], jnp.zeros((8, 128), F32)
        for r in range(2):
            mine = [(preq[0, p] == 2 * d + r) & (pused[0, p] > 0) for p in range(NPIECE)]
            top = jnp.full((8, 128), NEG, F32)
            for p in range(NPIECE):
                top = jnp.maximum(top, jnp.where(mine[p], pm[p], NEG))
            total = jnp.zeros((8, 128), F32)
            value = jnp.zeros((8, 128), F32)
            for p in range(NPIECE):
                factor = jnp.where(mine[p], jnp.exp(pm[p] - top), 0.0)
                total = total + factor * pz[p]
                value = value + factor * po[p]
            values.append(value)
            stats = jnp.where(lane8 == 2 * r, top, jnp.where(lane8 == 2 * r + 1, total, stats))
        do_[d] = jnp.concatenate(values, axis=0).astype(BF16)
        ds_[d] = stats
        return carry

    lax.fori_loop(0, NK, combine, 0)
    dor[kv] = do_[kv]
    dsr[kv] = ds_[kv]

    ring_hop(*hidden, 4)
    b1_wait(3)
    b1_send(4)
    a2_wait(1)
    a2_send(2)
    for d in range(2):
        ring_relayed(xb, hsr, 3, d)
    project_pair(3)
    for d in range(2):
        ring_relayed(xb, hsr, 4, d)
    project(at_hop(0, 4))

    low, high = pl.ds(REACH, REACH), pl.ds(D, REACH)
    start(kvb.at[low], kvb.at[pl.ds(D + REACH, REACH)], halo_s.at[0], halo_r.at[0], tprev)
    start(kvb.at[high], kvb.at[pl.ds(0, REACH)], halo_s.at[1], halo_r.at[1], tnext)

    def send_partial(o, carry):
        dev = rem(kv + o, NK)
        remote(do_.at[dev], dor.at[kv], dcs.at[dev], dcr.at[kv], (t, dev)).start()
        remote(ds_.at[dev], dsr.at[kv], dts.at[dev], dtr.at[kv], (t, dev)).start()
        return carry

    lax.fori_loop(1, NK, send_partial, 0)


    gi = rem(kv, 4)
    odd = rem(z, 2)
    q4 = z // 2

    def attend(b):
        r0 = pl.multiple_of(256 * b, 256)
        q = qb[pl.ds(r0, 256), :]
        keys = kvb[pl.ds(r0, 768), :]
        s = lax.dot_general(q, keys, (((1,), (1,)), ((), ())), preferred_element_type=F32)
        row = (r0 + lax.broadcasted_iota(jnp.int32, (256, 1), 0)).astype(F32)
        begin = jnp.max(jnp.where(ends <= row, ends, floor), axis=1, keepdims=True)
        end = jnp.min(jnp.where(ends > row, ends, 1e9), axis=1, keepdims=True)
        lo = jnp.maximum(begin, row - REACH)
        hi = jnp.minimum(end - 1.0, row + REACH)
        kid = (r0 - REACH + lax.broadcasted_iota(jnp.int32, (1, 768), 1)).astype(F32)
        s = jnp.where((kid >= lo) & (kid <= hi), s, NEG)
        m = jnp.max(s, axis=1, keepdims=True)
        w = jnp.exp(s - m)
        total = jnp.sum(w, axis=1, keepdims=True)
        o = jnp.dot(w.astype(BF16), keys, preferred_element_type=F32) / total
        lanes = lax.broadcasted_iota(jnp.int32, (128, 128), 1)
        turned = pltpu.roll(o[0:128], 64, 1)
        packed = jnp.where(lanes < 64, turned, o[128:256]).astype(BF16)
        ab[b] = packed
        slot = rem(q4 - b + 4, 4)

        @pl.when(b != q4)
        def _():
            remote(ab.at[b], ar.at[slot], aas.at[b], aar.at[slot], (t, 4 * b + gi)).start()

        @pl.when(b == q4)
        def _():
            ar[0] = packed

    def inner(i, carry):
        attend(1 + i)
        return carry

    def outer(i, carry):
        attend(3 * i)
        return carry

    b1_wait(4)
    hop_send(w2_block, x_at, xdev, w2s, w2r, 1, 2)
    hop_send(b2_block, x_at, xdev, b2s, b2r, 1, 2)
    lax.fori_loop(0, 2, inner, 0)
    hop_wait(w2_block, x_at, w2r, 1, 2)
    hop_send(w2_block, x_at, xdev, w2s, w2r, 2, 2)
    a2_wait(2)
    a2_send(3)
    arrived(kvb.at[pl.ds(D + REACH, REACH)], halo_r.at[0])
    arrived(kvb.at[pl.ds(0, REACH)], halo_r.at[1])
    lax.fori_loop(0, 2, outer, 0)

    for j in range(1, 4):
        arrived(ar.at[j], aar.at[j])
    local[2].wait()
    hop_wait(w2_block, x_at, w2r, 2, 2)

    lanes = lax.broadcasted_iota(jnp.int32, (128, 128), 1)
    for j in range(2):
        m0, m1 = ar[2 * j].astype(F32), ar[2 * j + 1].astype(F32)
        cols = pl.ds(128 * j, 128)
        atb[0, :, cols] = jnp.where(lanes < 64, m0, pltpu.roll(m1, 64, 1)).astype(BF16)
        atb[1, :, cols] = jnp.where(lanes < 64, pltpu.roll(m0, 64, 1), m1).astype(BF16)

    pair = (t, 2 * (z + 1 - 2 * odd) + c)

    def split(acc):
        low, high = acc[0:64], acc[64:128]
        first = c == 0
        return jnp.where(first, low, high), jnp.where(first, high, low)

    def heads(zz):
        return jnp.dot(atb[zz], wob[...].reshape(256, D), preferred_element_type=F32)

    ahead, other = split(heads(1 - odd))
    qso[1] = other.astype(BF16)
    start(qso.at[1], qsi.at[1], ps.at[1], pr.at[1], sib)
    keep, other = split(heads(odd))
    qso[0] = other.astype(BF16)
    start(qso.at[0], qsi.at[0], ps.at[0], pr.at[0], sib)
    a2_wait(3)
    a2_send(4)
    arrived(qsi.at[1], pr.at[1])
    qxo[...] = (ahead + qsi[1].astype(F32)).astype(BF16)
    start(qxo, qxi, ps.at[2], pr.at[2], pair)
    arrived(qsi.at[0], pr.at[0])
    keep = keep + qsi[0].astype(F32) + xb[own_rows, :].astype(F32)
    local[12].wait()
    local[13].wait()
    hop_wait(b2_block, x_at, b2r, 1, 2)
    hop_send(b2_block, x_at, xdev, b2s, b2r, 2, 2)
    arrived(qxi, pr.at[2])
    normed = layer_norm(keep + qxi[...].astype(F32), g1[...], b1[...]).astype(BF16)

    nb[pl.ds(pl.multiple_of(gi * 64, 64), 64), :] = normed

    def nrows(zz, core, h):
        return pl.ds(pl.multiple_of((2 * zz + core) * 64 + 32 * h, 32), 32)

    mine = nb.at[pl.ds(pl.multiple_of(gi * 64, 64), 64)]
    for h in range(2):
        ref = nb.at[nrows(odd, c, h)]
        start(ref, ref, ns.at[h], nr.at[h], pair)
    start(mine, mine, ns.at[2], nr.at[2], sib)

    arrived(nb.at[pl.ds(pl.multiple_of((2 * odd + 1 - c) * 64, 64), 64)], nr.at[2])
    for h in range(2):
        ref = nb.at[nrows(1 - odd, c, h)]
        arrived(ref, nr.at[h])
        start(ref, ref, ns.at[3 + h], nr.at[3 + h], sib)
    local[3].wait()
    local[4].wait()
    a2_wait(4)
    hop_wait(b2_block, x_at, b2r, 2, 2)

    def ffn(zz):
        rows = nb[pl.ds(pl.multiple_of(zz * 128, 128), 128), :]
        acc = jnp.zeros((128, D), F32)
        for j in range(4):
            units = gelu(jnp.dot(rows, upb[j], preferred_element_type=F32)).astype(BF16)
            acc = acc + jnp.dot(units, dnb[j], preferred_element_type=F32)
        return acc

    acc = ffn(odd)

    kept, other = split(acc)
    rso[0] = other.astype(BF16)
    start(rso.at[0], rsi.at[0], fs.at[0], fr.at[0], sib)
    for h in range(2):
        arrived(nb.at[nrows(1 - odd, 1 - c, h)], nr.at[3 + h])
    ahead, other = split(ffn(1 - odd))
    rso[1] = other.astype(BF16)
    start(rso.at[1], rsi.at[1], fs.at[1], fr.at[1], sib)
    arrived(rsi.at[1], fr.at[1])
    pxo[...] = (ahead + rsi[1].astype(F32)).astype(BF16)
    start(pxo, pxi, fs.at[2], fr.at[2], pair)

    def got_partial(o, carry):
        src = rem(kv + o, NK)
        arrived(dor.at[src], dcr.at[src])
        arrived(dsr.at[src], dtr.at[src])
        return carry

    lax.fori_loop(1, NK, got_partial, 0)
    stats = dsr[...]
    lane3 = lax.broadcasted_iota(jnp.int32, (NK, 8, 128), 2)

    def spread(at):
        a = jnp.sum(jnp.where(lane3 == at, stats, 0.0), axis=2, keepdims=True)
        b = jnp.sum(jnp.where(lane3 == at + 64, stats, 0.0), axis=2, keepdims=True)
        return jnp.where(lane3 < 64, a, b)

    done = []
    for r in range(2):
        top, total = spread(2 * r), spread(2 * r + 1)
        value = dor[:, 8 * r : 8 * r + 8, :].astype(F32)
        factor = jnp.exp(top - jnp.max(top, axis=0, keepdims=True))
        value = jnp.sum(factor * value, axis=0) / jnp.sum(factor * total, axis=0)
        done.append(jnp.concatenate([value[i : i + 1, :] for i in range(8)], axis=1))
    dec[...] = jnp.concatenate(done, axis=0).astype(BF16)

    arrived(rsi.at[0], fr.at[0])
    kept = kept + rsi[0].astype(F32) + nb[pl.ds(pl.multiple_of(gi * 64, 64), 64), :].astype(F32)
    arrived(pxi, fr.at[2])
    local[14].wait()
    local[15].wait()
    out[...] = layer_norm(kept + pxi[...].astype(F32), g2[...], b2[...]).astype(BF16)

    for copy in sent:
        copy.wait_send()

    def sent_small(o, carry):
        dev = rem(kv + o, NK)
        remote(dqs, dqb.at[kv], dqss.at[o - 1], dqsr.at[kv], (t, dev)).wait_send()
        remote(do_.at[dev], dor.at[kv], dcs.at[dev], dcr.at[kv], (t, dev)).wait_send()
        remote(ds_.at[dev], dsr.at[kv], dts.at[dev], dtr.at[kv], (t, dev)).wait_send()
        return carry

    lax.fori_loop(1, NK, sent_small, 0)

    def sent_heads(o, carry):
        b = rem(q4 + o, 4)
        slot = rem(q4 - b + 4, 4)
        remote(ab.at[b], ar.at[slot], aas.at[b], aar.at[slot], (t, 4 * b + gi)).wait_send()
        return carry

    lax.fori_loop(1, 4, sent_heads, 0)


def body(hid, wqkv, slen, wo, g1, b1, up, dn, g2, b2, dq, kvc, preq, pused):
    vm = pl.BlockSpec(memory_space=pltpu.VMEM)
    hbm = pl.BlockSpec(memory_space=pltpu.HBM)
    S = pltpu.SMEM
    dma = pltpu.SemaphoreType.DMA
    V = pltpu.VMEM
    return pl.pallas_call(
        kernel,
        out_shape=(
            jax.ShapeDtypeStruct((64, D), BF16),
            jax.ShapeDtypeStruct((2, D), BF16),
        ),
        in_specs=[hbm] * 14,
        out_specs=(vm, vm),
        scratch_shapes=[
            V((1, D), F32), V((1, D), F32), V((1, D), F32), V((1, D), F32), V((2, D), BF16),
            S((NSEG,), jnp.int32), S((1, NPIECE), jnp.int32), S((1, NPIECE), jnp.int32),
            V((D, D), BF16), V((4, 64, D), BF16), V((4, D, 256), BF16), V((4, 256, D), BF16),
            V((D + 2 * REACH, 128), BF16), V((D, 128), BF16), V((256, D), BF16), V((D, 256), BF16),
            V((4, 128, 128), BF16), V((4, 128, 128), BF16), V((2, 128, 256), BF16), V((256, D), BF16),
            V((2, 64, D), BF16), V((2, 64, D), BF16), V((64, D), BF16), V((64, D), BF16),
            V((2, 64, D), BF16), V((2, 64, D), BF16), V((64, D), BF16), V((64, D), BF16),
            V((2, NPIECE, 128, D), BF16),
            V((16, 128), F32), V((16, 128), BF16), V((NK, 16, 128), BF16),
            V((NPIECE, 8, 128), F32), V((NPIECE, 8, 128), F32), V((NPIECE, 8, 128), F32), V((48, 128), F32),
            V((NK, 16, 128), BF16), V((NK, 8, 128), F32), V((NK, 16, 128), BF16), V((NK, 8, 128), F32),
            dma((16,)),
            dma((16,)), dma((16,)), dma((17,)), dma((17,)),
            dma((9,)), dma((9,)), dma((3,)), dma((3,)), dma((8,)), dma((8,)),
            dma((8,)), dma((8,)), dma((4,)), dma((4,)), dma((8,)), dma((8,)), dma((4,)), dma((4,)), dma((3,)), dma((3,)),
            dma((2,)), dma((2,)),
            dma((4,)), dma((4,)),
            dma((NK,)), dma((NK,)), dma((NK,)), dma((NK,)), dma((NK,)), dma((NK,)),
            dma((5,)), dma((5,)), dma((3,)), dma((3,)),
        ],
        compiler_params=pltpu.CompilerParams(
            collective_id=0, has_side_effects=True, vmem_limit_bytes=65400 * 1024
        ),
    )(hid, jnp.transpose(wqkv, (1, 2, 0)), slen, wo, g1.reshape(1, D), b1.reshape(1, D), up, dn, g2.reshape(1, D), b2.reshape(1, D), dq, kvc, preq, pused)


def solution(mesh):
    rows = P(("tok", "kv"), None)
    placed = (
        rows, P(None, None, "kv"), P(), P("kv", None), P(), P(), P(None, "kv"), P("kv", None),
        P(), P(), rows, P(None, "tok", "kv", None, None), P("tok", "kv"), P("tok", "kv"),
    )
    return jax.shard_map(
        body, mesh=mesh, in_specs=placed, out_specs=(rows, rows), check_vma=False
    )
```

```python
import functools
import math

import jax
import jax.numpy as jnp
from jax import lax
from jax.experimental import pallas as pl
from jax.experimental.pallas import tpu as pltpu
from jax.sharding import PartitionSpec as P

MESH = pl.DeviceIdType.MESH
F32 = jnp.float32
BF16 = jnp.bfloat16
D = 1024
NZ = 8
NK = 16
NX = 4
NY = 8
NT = NX * NY
NSEG = 48
NPIECE = 6
REACH = 256
NEG = -1e30
EPS = 1e-5


def rem(value, count):
    return lax.rem(value, count)


def layer_norm(values, gain, bias):
    center = values - jnp.mean(values, axis=1, keepdims=True)
    spread = jnp.mean(center * center, axis=1, keepdims=True)
    return center * lax.rsqrt(spread + EPS) * gain + bias


def gelu(v):
    return v * (0.5 + 0.5 * lax.erf(v * (1.0 / math.sqrt(2.0))))


def kernel(
    hid, wqkv, slen_in, wo, g1_in, b1_in, up, dn, g2_in, b2_in, dq_in, kvc, preq_in, pused_in,
    out, dec,
    g1, b1, g2, b2, dq, slen, preq, pused,
    xb, wob, upb, dnb, kvb, qb, wcat, wtr, ab, ar, atb, nb, rso, rsi, pxo, pxi, qso, qsi, qxo, qxi, cache,
    dqf, dqs, dqb, po, pm, pz, gq, do_, ds_, dor, dsr,
    loc_sem,
    hzs, hzr, hss, hsr,
    seeds_s, seeds_r, a1s, a1r, a2s, a2r, b1s, b1r, b2s, b2r, w1s, w1r, w2s, w2r, ps, pr,
    halo_s, halo_r,
    aas, aar,
    dqss, dqsr, dcs, dcr, dts, dtr,
    ns, nr, fs, fr,
):
    t = lax.axis_index("tok")
    kv = lax.axis_index("kv")
    z, c = kv // 2, rem(kv, 2)
    y, x = t // NX, rem(t, NX)
    sib = (t, 2 * z + (1 - c))

    def remote(src, dst, ss, rs, dev):
        return pltpu.make_async_remote_copy(
            src_ref=src, dst_ref=dst, send_sem=ss, recv_sem=rs,
            device_id=dev, device_id_type=MESH,
        )

    sent = []

    def start(src, dst, ss, rs, dev):
        copy = remote(src, dst, ss, rs, dev)
        copy.start()
        sent.append(copy)

    def arrived(dst, rs):
        remote(dst, dst, loc_sem.at[0], rs, sib).wait_recv()

    own_rows = pl.ds(pl.multiple_of(kv * 64, 64), 64)
    local = [
        pltpu.make_async_copy(hid, xb.at[own_rows], loc_sem.at[0]),
        pltpu.make_async_copy(wqkv.at[0], wcat.at[pl.ds(0, 64)], loc_sem.at[1]),
        pltpu.make_async_copy(wo, wob.at[0], loc_sem.at[2]),
        pltpu.make_async_copy(up, upb.at[0], loc_sem.at[3]),
        pltpu.make_async_copy(dn, dnb.at[0], loc_sem.at[4]),
        pltpu.make_async_copy(kvc.at[:, 0], cache, loc_sem.at[5]),
        pltpu.make_async_copy(wqkv.at[1], wcat.at[pl.ds(128, 64)], loc_sem.at[6]),
        pltpu.make_async_copy(wqkv.at[2], wcat.at[pl.ds(192, 64)], loc_sem.at[7]),
        pltpu.make_async_copy(dq_in, dq, loc_sem.at[8]),
        pltpu.make_async_copy(slen_in, slen, loc_sem.at[9]),
        pltpu.make_async_copy(preq_in, preq, loc_sem.at[10]),
        pltpu.make_async_copy(pused_in, pused, loc_sem.at[11]),
        pltpu.make_async_copy(g1_in, g1, loc_sem.at[12]),
        pltpu.make_async_copy(b1_in, b1, loc_sem.at[13]),
        pltpu.make_async_copy(g2_in, g2, loc_sem.at[14]),
        pltpu.make_async_copy(b2_in, b2, loc_sem.at[15]),
    ]

    barrier = pltpu.get_barrier_semaphore()
    peers = [(t, rem(kv + o, NK)) for o in range(1, NK)]
    peers += [(y * NX + rem(x + o, NX), kv) for o in range(1, NX)]
    yup, ydown = (rem(y + 1, NY) * NX + x, kv), (rem(y + NY - 1, NY) * NX + x, kv)
    peers += [(rem(y + o, NY) * NX + x, kv) for o in range(1, NY)]
    tnext, tprev = (rem(t + 1, NT), kv), (rem(t + NT - 1, NT), kv)
    peers += [tnext, tprev]
    for peer in peers:
        pl.semaphore_signal(barrier, inc=1, device_id=peer, device_id_type=MESH)
    for i in (0, 8, 9):
        local[i].start()
    pl.semaphore_wait(barrier, len(peers))

    zdev = [(t, 2 * rem(z + 1, NZ) + c), (t, 2 * rem(z + NZ - 1, NZ) + c)]

    def at_hop(d, k):
        return rem(z + NZ - k, NZ) if d == 0 else rem(z + k, NZ)

    def part(zz, core, half=None):
        first = (2 * zz + core) * 64
        if half is None:
            return pl.ds(pl.multiple_of(first, 64), 64)
        return pl.ds(pl.multiple_of(first + 32 * half, 32), 32)

    def ring_send(buf, own, zs, zr, k, d):
        zz, i = at_hop(d, k - 1), d * 4 + k - 1
        rows = part(zz, c, d if k == 4 else None)
        src = own if k == 1 else buf.at[rows]
        start(src, buf.at[rows], zs.at[i], zr.at[i], zdev[d])

    def ring_first(buf, own, zs, zr, ss, sr):
        for d in range(2):
            ring_send(buf, own, zs, zr, 1, d)
        start(own, buf.at[own_rows], ss.at[8], sr.at[8], sib)

    def ring_hop(buf, own, zs, zr, ss, sr, k):
        for d in range(2):
            i = d * 4 + k - 1
            here = buf.at[part(at_hop(d, k), c, d if k == 4 else None)]
            arrived(here, zr.at[i])
            if k < 4:
                ring_send(buf, own, zs, zr, k + 1, d)
            start(here, here, ss.at[i], sr.at[i], sib)

    def ring_relayed(buf, sr, k, d):
        arrived(buf.at[part(at_hop(d, k), 1 - c, d if k == 4 else None)], sr.at[d * 4 + k - 1])

    hidden = (xb, hid, hzs, hzr, hss, hsr)
    sib_rows = pl.ds(pl.multiple_of((2 * z + 1 - c) * 64, 64), 64)


    up_rows = pl.ds(pl.multiple_of(t * 32, 32), 32)

    def dn_block(xx, yy, half=None):
        if half is None:
            cols = pl.ds(pl.multiple_of(512 * (yy // 4), 512), 512)
        else:
            cols = pl.ds(pl.multiple_of(512 * (yy // 4) + 256 * half, 256), 256)
        return pl.ds(pl.multiple_of(64 * xx + 16 * rem(yy, 4), 16), 16), cols

    def wo_block(xx, yy):
        return (
            pl.ds(pl.multiple_of(16 * rem(yy, 4), 16), 16),
            pl.ds(pl.multiple_of(256 * xx + 128 * (yy // 4), 128), 128),
        )

    for i in (1, 6, 7, 10, 11, 5, 2, 3, 4, 12, 13, 14, 15):
        local[i].start()

    sign = 2 * rem(z, 2) - 1
    dr, dcol = dn_block(x, y)
    wr, wcol = wo_block(x, y)
    for j in range(1, 4):
        dev = (t, 2 * rem(z + NZ + sign * (j if j != 2 else -2), NZ) + c)
        start(wo.at[wr, wcol], wob.at[j, wr, wcol], seeds_s.at[j + 5], seeds_r.at[j + 5], dev)
        start(up.at[up_rows, :], upb.at[j, up_rows, :], seeds_s.at[j - 1], seeds_r.at[j - 1], dev)
        start(dn.at[dr, dcol], dnb.at[j, dr, dcol], seeds_s.at[j + 2], seeds_r.at[j + 2], dev)

    ring_first(*hidden)

    local[8].wait()
    qf = dq[...].astype(F32)
    for i in range(8):
        dqf[pl.ds(2 * i, 2), :] = qf[:, 128 * i : 128 * i + 128]
    dqs[...] = dqf[...].astype(BF16)
    dqb[kv] = dqs[...]

    def send_query(o, carry):
        dev = rem(kv + o, NK)
        remote(dqs, dqb.at[kv], dqss.at[o - 1], dqsr.at[kv], (t, dev)).start()
        return carry

    lax.fori_loop(1, NK, send_query, 0)

    local[9].wait()
    first = t * D
    lane = lax.broadcasted_iota(jnp.int32, (1, 128), 1)
    ends = jnp.zeros((1, 128), jnp.int32)

    def add_len(i, ends):
        return ends + jnp.where(lane >= i, slen[i], 0)

    ends = (lax.fori_loop(0, NSEG, add_len, ends) - first).astype(F32)
    floor = (-first).astype(F32)

    wcat[pl.ds(64, 64), :] = jnp.zeros((64, D), BF16)
    for i in (1, 6, 7):
        local[i].wait()

    for i in range(4):
        rows = pl.ds(256 * i, 256)
        wtr[rows, :] = wcat[:, rows].astype(F32).T.astype(BF16)

    def project(zz):
        rows = pl.ds(pl.multiple_of(zz * 128, 128), 128)
        res = jnp.dot(xb[rows, :], wtr[...], preferred_element_type=F32).astype(BF16)
        qb[rows, :] = res[:, 0:128] * 0.125
        kvb[pl.ds(pl.multiple_of(zz * 128 + REACH, 128), 128), :] = res[:, 128:256]

    def project_pair(k):
        def one(d, carry):
            project(jnp.where(d == 0, rem(z + NZ - k, NZ), rem(z + k, NZ)))
            return carry

        lax.fori_loop(0, 2, one, 0)

    ring_hop(*hidden, 1)

    slots = pl.ds(1, 3)
    xdev = [(y * NX + rem(x + 1, NX), kv), (y * NX + rem(x + NX - 1, NX), kv)]
    ydev = [yup, ydown]

    def y_at(d, k):
        return rem(y + NY - k, NY) if d == 0 else rem(y + k, NY)

    def x_at(d, k):
        return rem(x + NX - k, NX) if d == 0 else rem(x + k, NX)

    def a2_block(yy, half):
        if half is None:
            return upb.at[slots, pl.ds(pl.multiple_of(yy * 128, 128), 128), :]
        return upb.at[slots, pl.ds(pl.multiple_of(yy * 128 + 64 * half, 64), 64), :]

    def b1_block(yy, half):
        r, cc = dn_block(x, yy, half)
        return dnb.at[slots, r, cc]

    def w1_block(yy, half):
        r, cc = wo_block(x, yy)
        return wob.at[slots, r, cc]

    def b2_block(xx, half):
        if half is None:
            return dnb.at[slots, pl.ds(pl.multiple_of(64 * xx, 64), 64), :]
        return dnb.at[slots, pl.ds(pl.multiple_of(64 * xx + 32 * half, 32), 32), :]

    def w2_block(xx, half):
        cols = pl.ds(pl.multiple_of(256 * xx, 256), 256)
        if half is None:
            return wob.at[slots, :, cols]
        return wob.at[slots, pl.ds(32 * half, 32), cols]

    def hop_send(block, at, devs, ss, sr, k, hops, whole=False):
        for d in range(2):
            if whole and k == hops and d == 1:
                continue
            ref = block(at(d, k - 1), d if k == hops and not whole else None)
            start(ref, ref, ss.at[d * hops + k - 1], sr.at[d * hops + k - 1], devs[d])

    def hop_wait(block, at, sr, k, hops, whole=False):
        for d in range(2):
            if whole and k == hops and d == 1:
                continue
            arrived(block(at(d, k), d if k == hops and not whole else None), sr.at[d * hops + k - 1])

    def a2_send(k):
        hop_send(a2_block, y_at, ydev, a2s, a2r, k, 4)

    def a2_wait(k):
        hop_wait(a2_block, y_at, a2r, k, 4)

    def b1_send(k):
        hop_send(b1_block, y_at, ydev, b1s, b1r, k, 4)

    def b1_wait(k):
        hop_wait(b1_block, y_at, b1r, k, 4)

    for j in range(1, 4):
        arrived(wob.at[j, wr, wcol], seeds_r.at[j + 5])
        arrived(upb.at[j, up_rows, :], seeds_r.at[j - 1])
        arrived(dnb.at[j, dr, dcol], seeds_r.at[j + 2])
    seed = upb.at[slots, up_rows, :]
    for o in range(1, NX):
        start(seed, seed, a1s.at[o - 1], a1r.at[o - 1], (y * NX + rem(x + o, NX), kv))
    shard = wob.at[slots, wr, wcol]
    for o in range(1, NY):
        start(shard, shard, w1s.at[o - 1], w1r.at[o - 1], (rem(y + o, NY) * NX + x, kv))
    b1_send(1)
    local[0].wait()
    arrived(xb.at[sib_rows], hsr.at[8])
    project(z)

    ring_hop(*hidden, 2)
    for o in range(1, NX):
        rows = pl.ds(pl.multiple_of((y * NX + rem(x + NX - o, NX)) * 32, 32), 32)
        arrived(upb.at[slots, rows, :], a1r.at[o - 1])
    a2_send(1)
    b1_wait(1)
    b1_send(2)
    for d in range(2):
        ring_relayed(xb, hsr, 1, d)
    project_pair(1)

    def got_query(o, carry):
        src = rem(kv + o, NK)
        arrived(dqb.at[src], dqsr.at[src])
        return carry

    lax.fori_loop(1, NK, got_query, 0)
    local[10].wait()
    local[11].wait()
    row48 = lax.broadcasted_iota(jnp.int32, (48, 1), 0)
    target = 2 * rem(row48, 8)
    for p in range(NPIECE):
        n = preq[0, p]
        target = target + jnp.where(row48 // 8 == p, 16 * (n // 2) + rem(n, 2), 0)
    col256 = lax.broadcasted_iota(jnp.int32, (48, 256), 1)
    select = (col256 == target).astype(F32).astype(BF16)
    gq[...] = jnp.dot(select, dqb[...].reshape(256, 128), preferred_element_type=F32)
    local[5].wait()
    head16 = lax.broadcasted_iota(jnp.int32, (16, 128), 0)
    lane16 = lax.broadcasted_iota(jnp.int32, (16, 128), 1)
    masks = [head16 == 2 * i + lane16 // 64 for i in range(8)]

    def piece(p, carry):
        g = gq[pl.ds(pl.multiple_of(8 * p, 8), 8), :]
        qbd = jnp.concatenate(
            [jnp.where(masks[i], g[i : i + 1, :], 0.0) for i in range(8)], axis=1
        ).astype(BF16)
        u = lax.dot_general(
            qbd, cache[0, p], (((1,), (1,)), ((), ())), preferred_element_type=F32
        ) * 0.125
        live = lane16 < pused[0, p]
        u = jnp.where(live, u, NEG)
        m = jnp.max(u, axis=1, keepdims=True)
        e = jnp.where(live, jnp.exp(u - m), 0.0)
        s = jnp.sum(e, axis=1, keepdims=True)
        o = jnp.dot(e.astype(BF16), cache[1, p], preferred_element_type=F32)
        for i in range(8):
            po[p, i : i + 1, :] = jnp.sum(
                jnp.where(masks[i], o[:, 128 * i : 128 * i + 128], 0.0), axis=0, keepdims=True
            )
            pm[p, i : i + 1, :] = jnp.sum(jnp.where(masks[i], m, 0.0), axis=0, keepdims=True)
            pz[p, i : i + 1, :] = jnp.sum(jnp.where(masks[i], s, 0.0), axis=0, keepdims=True)
        return carry

    lax.fori_loop(0, NPIECE, piece, 0)

    ring_hop(*hidden, 3)
    for o in range(1, NY):
        arrived(w1_block(rem(y + NY - o, NY), None), w1r.at[o - 1])
    part_cols = w2_block(x, None)
    for o in range(1, NX):
        start(part_cols, part_cols, w2s.at[o - 1], w2r.at[o - 1], (y * NX + rem(x + o, NX), kv))
    b1_wait(2)
    b1_send(3)
    for d in range(2):
        ring_relayed(xb, hsr, 2, d)
    project_pair(2)
    lane8 = rem(lax.broadcasted_iota(jnp.int32, (8, 128), 1), 64)

    def combine(d, carry):
        values, stats = [], jnp.zeros((8, 128), F32)
        for r in range(2):
            mine = [(preq[0, p] == 2 * d + r) & (pused[0, p] > 0) for p in range(NPIECE)]
            top = jnp.full((8, 128), NEG, F32)
            for p in range(NPIECE):
                top = jnp.maximum(top, jnp.where(mine[p], pm[p], NEG))
            total = jnp.zeros((8, 128), F32)
            value = jnp.zeros((8, 128), F32)
            for p in range(NPIECE):
                factor = jnp.where(mine[p], jnp.exp(pm[p] - top), 0.0)
                total = total + factor * pz[p]
                value = value + factor * po[p]
            values.append(value)
            stats = jnp.where(lane8 == 2 * r, top, jnp.where(lane8 == 2 * r + 1, total, stats))
        do_[d] = jnp.concatenate(values, axis=0).astype(BF16)
        ds_[d] = stats
        return carry

    lax.fori_loop(0, NK, combine, 0)
    dor[kv] = do_[kv]
    dsr[kv] = ds_[kv]

    ring_hop(*hidden, 4)
    b1_wait(3)
    b1_send(4)
    a2_wait(1)
    a2_send(2)
    for d in range(2):
        ring_relayed(xb, hsr, 3, d)
    project_pair(3)
    for d in range(2):
        ring_relayed(xb, hsr, 4, d)
    project(at_hop(0, 4))

    low, high = pl.ds(REACH, REACH), pl.ds(D, REACH)
    start(kvb.at[low], kvb.at[pl.ds(D + REACH, REACH)], halo_s.at[0], halo_r.at[0], tprev)
    start(kvb.at[high], kvb.at[pl.ds(0, REACH)], halo_s.at[1], halo_r.at[1], tnext)

    def send_partial(o, carry):
        dev = rem(kv + o, NK)
        remote(do_.at[dev], dor.at[kv], dcs.at[dev], dcr.at[kv], (t, dev)).start()
        remote(ds_.at[dev], dsr.at[kv], dts.at[dev], dtr.at[kv], (t, dev)).start()
        return carry

    lax.fori_loop(1, NK, send_partial, 0)


    gi = rem(kv, 4)
    odd = rem(z, 2)
    q4 = z // 2

    def holder(b):
        step = rem(sign * (b - q4) + 4, 4)
        turn = (step - 1) * (step - 2) // 2
        slot = 1 + 2 * (step - 1) - 3 * turn
        ahead = 1 + 2 * (step - 1) - 7 * turn
        return rem(slot + 4, 4), (t, 2 * rem(z + 2 * NZ + sign * ahead, NZ) + c)

    def attend(b):
        r0 = pl.multiple_of(256 * b, 256)
        q = qb[pl.ds(r0, 256), :]
        keys = kvb[pl.ds(r0, 768), :]
        s = lax.dot_general(q, keys, (((1,), (1,)), ((), ())), preferred_element_type=F32)
        row = (r0 + lax.broadcasted_iota(jnp.int32, (256, 1), 0)).astype(F32)
        begin = jnp.max(jnp.where(ends <= row, ends, floor), axis=1, keepdims=True)
        end = jnp.min(jnp.where(ends > row, ends, 1e9), axis=1, keepdims=True)
        lo = jnp.maximum(begin, row - REACH)
        hi = jnp.minimum(end - 1.0, row + REACH)
        kid = (r0 - REACH + lax.broadcasted_iota(jnp.int32, (1, 768), 1)).astype(F32)
        s = jnp.where((kid >= lo) & (kid <= hi), s, NEG)
        m = jnp.max(s, axis=1, keepdims=True)
        w = jnp.exp(s - m)
        total = jnp.sum(w, axis=1, keepdims=True)
        o = jnp.dot(w.astype(BF16), keys, preferred_element_type=F32) / total
        lanes = lax.broadcasted_iota(jnp.int32, (128, 128), 1)
        turned = pltpu.roll(o[0:128], 64, 1)
        packed = jnp.where(lanes < 64, turned, o[128:256]).astype(BF16)
        ab[b] = packed
        slot, dev = holder(b)

        @pl.when(b != q4)
        def _():
            remote(ab.at[b], ar.at[slot], aas.at[b], aar.at[slot], dev).start()

        @pl.when(b == q4)
        def _():
            ar[0] = packed

    def inner(i, carry):
        attend(1 + i)
        return carry

    def outer(i, carry):
        attend(3 * i)
        return carry

    b1_wait(4)
    hop_send(b2_block, x_at, xdev, b2s, b2r, 1, 2)
    lax.fori_loop(0, 2, inner, 0)
    a2_wait(2)
    a2_send(3)
    arrived(kvb.at[pl.ds(D + REACH, REACH)], halo_r.at[0])
    arrived(kvb.at[pl.ds(0, REACH)], halo_r.at[1])
    lax.fori_loop(0, 2, outer, 0)

    for j in range(1, 4):
        arrived(ar.at[j], aar.at[j])
    local[2].wait()
    for o in range(1, NX):
        arrived(w2_block(rem(x + NX - o, NX), None), w2r.at[o - 1])

    lanes = lax.broadcasted_iota(jnp.int32, (128, 128), 1)
    for j in range(2):
        m0, m1 = ar[2 * j].astype(F32), ar[2 * j + 1].astype(F32)
        cols = pl.ds(128 * j, 128)
        atb[0, :, cols] = jnp.where(lanes < 64, m0, pltpu.roll(m1, 64, 1)).astype(BF16)
        atb[1, :, cols] = jnp.where(lanes < 64, pltpu.roll(m0, 64, 1), m1).astype(BF16)

    pair = (t, 2 * (z + 1 - 2 * odd) + c)

    def split(acc):
        low, high = acc[0:64], acc[64:128]
        first = c == 0
        return jnp.where(first, low, high), jnp.where(first, high, low)

    def heads(zz):
        return jnp.dot(atb[zz], wob[...].reshape(256, D), preferred_element_type=F32)

    ahead, other = split(heads(1 - odd))
    qso[1] = other.astype(BF16)
    start(qso.at[1], qsi.at[1], ps.at[1], pr.at[1], sib)
    keep, other = split(heads(odd))
    qso[0] = other.astype(BF16)
    start(qso.at[0], qsi.at[0], ps.at[0], pr.at[0], sib)
    a2_wait(3)
    a2_send(4)
    arrived(qsi.at[1], pr.at[1])
    qxo[...] = (ahead + qsi[1].astype(F32)).astype(BF16)
    start(qxo, qxi, ps.at[2], pr.at[2], pair)
    arrived(qsi.at[0], pr.at[0])
    keep = keep + qsi[0].astype(F32) + xb[own_rows, :].astype(F32)
    local[12].wait()
    local[13].wait()
    hop_wait(b2_block, x_at, b2r, 1, 2)
    hop_send(b2_block, x_at, xdev, b2s, b2r, 2, 2)
    arrived(qxi, pr.at[2])
    normed = layer_norm(keep + qxi[...].astype(F32), g1[...], b1[...]).astype(BF16)

    nb[pl.ds(pl.multiple_of(gi * 64, 64), 64), :] = normed

    def nrows(zz, core, h):
        return pl.ds(pl.multiple_of((2 * zz + core) * 64 + 32 * h, 32), 32)

    mine = nb.at[pl.ds(pl.multiple_of(gi * 64, 64), 64)]
    for h in range(2):
        ref = nb.at[nrows(odd, c, h)]
        start(ref, ref, ns.at[h], nr.at[h], pair)
    start(mine, mine, ns.at[2], nr.at[2], sib)

    arrived(nb.at[pl.ds(pl.multiple_of((2 * odd + 1 - c) * 64, 64), 64)], nr.at[2])
    for h in range(2):
        ref = nb.at[nrows(1 - odd, c, h)]
        arrived(ref, nr.at[h])
        start(ref, ref, ns.at[3 + h], nr.at[3 + h], sib)
    local[3].wait()
    local[4].wait()
    a2_wait(4)
    hop_wait(b2_block, x_at, b2r, 2, 2)

    def ffn(zz):
        rows = nb[pl.ds(pl.multiple_of(zz * 128, 128), 128), :]
        acc = jnp.zeros((128, D), F32)
        for j in range(4):
            units = gelu(jnp.dot(rows, upb[j], preferred_element_type=F32)).astype(BF16)
            acc = acc + jnp.dot(units, dnb[j], preferred_element_type=F32)
        return acc

    for h in range(2):
        arrived(nb.at[nrows(1 - odd, 1 - c, h)], nr.at[3 + h])
    ahead, other = split(ffn(1 - odd))
    rso[1] = other.astype(BF16)
    start(rso.at[1], rsi.at[1], fs.at[1], fr.at[1], sib)
    kept, other = split(ffn(odd))
    rso[0] = other.astype(BF16)
    start(rso.at[0], rsi.at[0], fs.at[0], fr.at[0], sib)
    arrived(rsi.at[1], fr.at[1])
    pxo[...] = (ahead + rsi[1].astype(F32)).astype(BF16)
    start(pxo, pxi, fs.at[2], fr.at[2], pair)

    def got_partial(o, carry):
        src = rem(kv + o, NK)
        arrived(dor.at[src], dcr.at[src])
        arrived(dsr.at[src], dtr.at[src])
        return carry

    lax.fori_loop(1, NK, got_partial, 0)
    stats = dsr[...]
    lane3 = lax.broadcasted_iota(jnp.int32, (NK, 8, 128), 2)

    def spread(at):
        a = jnp.sum(jnp.where(lane3 == at, stats, 0.0), axis=2, keepdims=True)
        b = jnp.sum(jnp.where(lane3 == at + 64, stats, 0.0), axis=2, keepdims=True)
        return jnp.where(lane3 < 64, a, b)

    done = []
    for r in range(2):
        top, total = spread(2 * r), spread(2 * r + 1)
        value = dor[:, 8 * r : 8 * r + 8, :].astype(F32)
        factor = jnp.exp(top - jnp.max(top, axis=0, keepdims=True))
        value = jnp.sum(factor * value, axis=0) / jnp.sum(factor * total, axis=0)
        done.append(jnp.concatenate([value[i : i + 1, :] for i in range(8)], axis=1))
    dec[...] = jnp.concatenate(done, axis=0).astype(BF16)

    arrived(rsi.at[0], fr.at[0])
    kept = kept + rsi[0].astype(F32) + nb[pl.ds(pl.multiple_of(gi * 64, 64), 64), :].astype(F32)
    arrived(pxi, fr.at[2])
    local[14].wait()
    local[15].wait()
    out[...] = layer_norm(kept + pxi[...].astype(F32), g2[...], b2[...]).astype(BF16)

    for copy in sent:
        copy.wait_send()

    def sent_small(o, carry):
        dev = rem(kv + o, NK)
        remote(dqs, dqb.at[kv], dqss.at[o - 1], dqsr.at[kv], (t, dev)).wait_send()
        remote(do_.at[dev], dor.at[kv], dcs.at[dev], dcr.at[kv], (t, dev)).wait_send()
        remote(ds_.at[dev], dsr.at[kv], dts.at[dev], dtr.at[kv], (t, dev)).wait_send()
        return carry

    lax.fori_loop(1, NK, sent_small, 0)

    def sent_heads(o, carry):
        b = rem(q4 + o, 4)
        slot, dev = holder(b)
        remote(ab.at[b], ar.at[slot], aas.at[b], aar.at[slot], dev).wait_send()
        return carry

    lax.fori_loop(1, 4, sent_heads, 0)


def body(hid, wqkv, slen, wo, g1, b1, up, dn, g2, b2, dq, kvc, preq, pused):
    vm = pl.BlockSpec(memory_space=pltpu.VMEM)
    hbm = pl.BlockSpec(memory_space=pltpu.HBM)
    S = pltpu.SMEM
    dma = pltpu.SemaphoreType.DMA
    V = pltpu.VMEM
    return pl.pallas_call(
        kernel,
        out_shape=(
            jax.ShapeDtypeStruct((64, D), BF16),
            jax.ShapeDtypeStruct((2, D), BF16),
        ),
        in_specs=[hbm] * 14,
        out_specs=(vm, vm),
        scratch_shapes=[
            V((1, D), F32), V((1, D), F32), V((1, D), F32), V((1, D), F32), V((2, D), BF16),
            S((NSEG,), jnp.int32), S((1, NPIECE), jnp.int32), S((1, NPIECE), jnp.int32),
            V((D, D), BF16), V((4, 64, D), BF16), V((4, D, 256), BF16), V((4, 256, D), BF16),
            V((D + 2 * REACH, 128), BF16), V((D, 128), BF16), V((256, D), BF16), V((D, 256), BF16),
            V((4, 128, 128), BF16), V((4, 128, 128), BF16), V((2, 128, 256), BF16), V((256, D), BF16),
            V((2, 64, D), BF16), V((2, 64, D), BF16), V((64, D), BF16), V((64, D), BF16),
            V((2, 64, D), BF16), V((2, 64, D), BF16), V((64, D), BF16), V((64, D), BF16),
            V((2, NPIECE, 128, D), BF16),
            V((16, 128), F32), V((16, 128), BF16), V((NK, 16, 128), BF16),
            V((NPIECE, 8, 128), F32), V((NPIECE, 8, 128), F32), V((NPIECE, 8, 128), F32), V((48, 128), F32),
            V((NK, 16, 128), BF16), V((NK, 8, 128), F32), V((NK, 16, 128), BF16), V((NK, 8, 128), F32),
            dma((16,)),
            dma((8,)), dma((8,)), dma((9,)), dma((9,)),
            dma((9,)), dma((9,)), dma((3,)), dma((3,)), dma((8,)), dma((8,)),
            dma((8,)), dma((8,)), dma((4,)), dma((4,)), dma((8,)), dma((8,)), dma((4,)), dma((4,)), dma((3,)), dma((3,)),
            dma((2,)), dma((2,)),
            dma((4,)), dma((4,)),
            dma((NK,)), dma((NK,)), dma((NK,)), dma((NK,)), dma((NK,)), dma((NK,)),
            dma((5,)), dma((5,)), dma((3,)), dma((3,)),
        ],
        compiler_params=pltpu.CompilerParams(
            collective_id=0, has_side_effects=True, vmem_limit_bytes=65400 * 1024
        ),
    )(hid, jnp.transpose(wqkv, (1, 2, 0)), slen, wo, g1.reshape(1, D), b1.reshape(1, D), up, dn, g2.reshape(1, D), b2.reshape(1, D), dq, kvc, preq, pused)


def solution(mesh):
    rows = P(("tok", "kv"), None)
    placed = (
        rows, P(None, None, "kv"), P(), P("kv", None), P(), P(), P(None, "kv"), P("kv", None),
        P(), P(), rows, P(None, "tok", "kv", None, None), P("tok", "kv"), P("tok", "kv"),
    )
    return jax.shard_map(
        body, mesh=mesh, in_specs=placed, out_specs=(rows, rows), check_vma=False
    )
```
